32 devices in a mesh: tile: 8 (over y, x, core), head: 4 (over z).
Axes of the slice: x: 2, y: 2, z: 4, core: 2. Of those that a mesh axis runs over, the one named last changes fastest.
Arguments:
- tokens: bfloat16 [2048, 384], P('tile'), may hold values from -6 to 6
- ln_gain: float32 [384], replicated, may hold values from 0.1 to 1.9
- qkv_weight: bfloat16 [3, 768, 384], P(None, 'head'), may hold values from -0.3125 to 0.3125
- query_pool: bfloat16 [4, 768], P(None, 'head'), may hold values from -3 to 3
- key_pool: bfloat16 [16, 768], P(None, 'head'), may hold values from -1.5 to 1.5
- value_pool: bfloat16 [16, 768], P(None, 'head'), may hold values from -1.5 to 1.5
- proj_weight: bfloat16 [768, 768], P('head'), may hold values from -0.21875 to 0.21875
- skip_weight: bfloat16 [768, 384], P('head'), may hold values from -0.3125 to 0.3125
- cotangent: bfloat16 [512, 768], P('tile', 'head'), may hold values from -6 to 6
Outputs:
- block_out: bfloat16 [512, 768], P('tile', 'head')
- input_grad: bfloat16 [2048, 384], P('tile')
- qkv_grad: float32 [3, 768, 384], P(None, 'head')
- proj_grad: float32 [768, 768], P('head')
The draws below stay inside these ranges and needn't reach their ends.
All inputs are finite; a program needn't handle non-finite values.
Results may differ from the reference program's by a relative error of at most 0.02.
Values may be sent and summed in bfloat16 or wider, within the bound.
A program may use at most 64 MiB of HBM per device.

```python
import jax
import jax.numpy as jnp
from jax import lax

C_IN = 384
C_OUT = 768
HEADS = 8
HEAD_DIM = 96
TILE_H = 8
TILE_W = 32
TOKENS = 2048
N_TILE = 8


def shard_levels(stream_key, extent, pieces, low, top_value):
    def one(dim, parts):
        heights = jax.random.uniform(jax.random.fold_in(jax.random.fold_in(stream_key, 6), dim), (parts,), jnp.float32, low / len(pieces), top_value / len(pieces))
        return jnp.repeat(jnp.exp(heights), extent[dim] // parts).reshape((-1,) + (1,) * (len(extent) - dim - 1))

    loudness = one(*pieces[0])
    for cut in pieces[1:]:
        loudness = loudness * one(*cut)
    return loudness


def noise(key, extent, scale, limit, shards=(), held_as=jnp.bfloat16):
    entries = jax.random.normal(key, extent, jnp.float32) * scale
    if len(shards) > 0:
        entries = shard_levels(key, extent, shards, -0.22, 0.18) * entries
    return jnp.clip(entries, min=-limit, max=limit).astype(held_as)


def setup_inputs(seed: int = 0) -> dict:
    streams_of = jax.random.split(jax.random.key(seed), 10)
    return {
        "tokens": noise(streams_of[0], (TOKENS, C_IN), 1.0, 6.0, ((0, 8),)),
        "ln_gain": jnp.clip(1.0 + 0.18 * jax.random.normal(streams_of[1], (C_IN,), jnp.float32), 0.1, 1.9),
        "qkv_weight": noise(streams_of[2], (3, C_OUT, C_IN), C_IN ** -0.5, 0.3125, ((1, 4),)),
        "query_pool": noise(streams_of[3], (4, C_OUT), 4 ** -0.5, 3.0, ((1, 4),)),
        "key_pool": noise(streams_of[4], (16, C_OUT), 16 ** -0.5, 1.5, ((1, 4),)),
        "value_pool": noise(streams_of[5], (16, C_OUT), 16 ** -0.5, 1.5, ((1, 4),)),
        "proj_weight": noise(streams_of[6], (C_OUT, C_OUT), C_OUT ** -0.5, 0.21875, ((0, 4),)),
        "skip_weight": noise(streams_of[7], (C_OUT, C_IN), C_IN ** -0.5, 0.3125, ((0, 4),)),
        "cotangent": noise(streams_of[8], (TOKENS // 4, C_OUT), 1.0, 6.0, ((0, 8), (1, 4))),
    }


EPSILON = 1e-06

def normalize(tokens):
    values_in = tokens.astype(jnp.float32)
    center = values_in - lax.optimization_barrier(jnp.mean(values_in, axis=-1, keepdims=True))
    inv_std = lax.rsqrt(lax.optimization_barrier(jnp.mean(center * center, axis=-1, keepdims=True)) + EPSILON)
    return (center * inv_std, inv_std)

def pool_field(feature, weight, stride):
    channels = feature.shape[-1]
    cells_grid = feature.reshape(-1, TILE_H // stride, stride, TILE_W // stride, stride, channels)
    kernel = weight.astype(jnp.float32).reshape(stride, stride, channels)
    return jnp.einsum('fiajbc,abc->fijc', cells_grid, kernel).reshape(-1, channels)

def spread_field(upstream, weight, stride):
    channels = upstream.shape[-1]
    cells_grid = upstream.reshape(-1, TILE_H // stride, TILE_W // stride, channels)
    kernel = weight.astype(jnp.float32).reshape(stride, stride, channels)
    return jnp.einsum('fijc,abc->fiajbc', cells_grid, kernel).reshape(-1, channels)

def mean_pool(tokens):
    channels = tokens.shape[-1]
    cells_grid = tokens.astype(jnp.float32).reshape(-1, TILE_H // 2, 2, TILE_W // 2, 2, channels)
    return lax.optimization_barrier(jnp.sum(cells_grid, axis=(2, 4))).reshape(-1, channels) * 0.25

def expand_rows(upstream):
    channels = upstream.shape[-1]
    cells_grid = upstream.reshape(-1, TILE_H // 2, 1, TILE_W // 2, 1, channels)
    cells_grid = jnp.broadcast_to(cells_grid, (cells_grid.shape[0], TILE_H // 2, 2, TILE_W // 2, 2, channels))
    return cells_grid.reshape(-1, channels)

def norm_back(upstream, unit_rows, inv_std, ln_gain):
    scaled = upstream * ln_gain
    return inv_std * (scaled - lax.optimization_barrier(jnp.mean(scaled, axis=-1, keepdims=True)) - unit_rows * lax.optimization_barrier(jnp.mean(scaled * unit_rows, axis=-1, keepdims=True)))

def attend(queries, grad_rows, key_rows, value_rows):
    scale = HEAD_DIM ** (-0.5)
    scores = jnp.dot(queries, key_rows.T, preferred_element_type=jnp.float32) * scale
    exp_scores = jnp.exp(scores)
    row_total = lax.optimization_barrier(jnp.sum(exp_scores, axis=-1, keepdims=True))
    attn_probs = (exp_scores / row_total).astype(jnp.bfloat16)
    out_rows = (jnp.dot(attn_probs, value_rows, preferred_element_type=jnp.float32) + queries.astype(jnp.float32)).astype(jnp.bfloat16)
    dprobs = jnp.dot(grad_rows, value_rows.T, preferred_element_type=jnp.float32)
    probs_wide = attn_probs.astype(jnp.float32)
    row_delta = lax.optimization_barrier(jnp.sum(probs_wide * dprobs, axis=-1, keepdims=True))
    d_scores = (scale * probs_wide * (dprobs - row_delta)).astype(jnp.bfloat16)
    dquery = jnp.dot(d_scores, key_rows, preferred_element_type=jnp.float32) + grad_rows.astype(jnp.float32)
    key_grad = jnp.dot(d_scores.T, queries, preferred_element_type=jnp.float32)
    value_grad = jnp.dot(attn_probs.T, grad_rows, preferred_element_type=jnp.float32)
    return (out_rows, dquery, key_grad, value_grad, row_total[:, 0], row_delta[:, 0])

def head_pass(operands):
    queries, grad_rows, key_rows, value_rows = operands

    def scan_step(accum, query_block):
        out_rows, dquery, key_grad, value_grad, row_total, row_delta = attend(query_block[0], query_block[1], key_rows, value_rows)
        return ((accum[0] + key_grad, accum[1] + value_grad), (out_rows, dquery))
    zero_grad = jnp.zeros(key_rows.shape, jnp.float32)
    accum, results = lax.scan(scan_step, (zero_grad, zero_grad), (queries, grad_rows))
    return (results[0], results[1], accum[0], accum[1])

def split_heads(rows_in, blocks):
    return rows_in.reshape(rows_in.shape[0], HEADS, HEAD_DIM).transpose(1, 0, 2).reshape(HEADS, blocks, -1, HEAD_DIM)

def join_heads(stacked):
    return stacked.reshape(HEADS, -1, HEAD_DIM).transpose(1, 0, 2).reshape(-1, C_OUT)

def reference(tokens, ln_gain, qkv_weight, query_pool, key_pool, value_pool, proj_weight, skip_weight, cotangent):
    unit_rows, inv_std = normalize(tokens)
    normed = (unit_rows * ln_gain).astype(jnp.bfloat16)
    projected = [jnp.dot(normed, qkv_weight[which].T, preferred_element_type=jnp.float32) for which in range(3)]
    query_pooled = pool_field(projected[0], query_pool, 2).astype(jnp.bfloat16)
    key_pooled = pool_field(projected[1], key_pool, 4).astype(jnp.bfloat16)
    value_pooled = pool_field(projected[2], value_pool, 4).astype(jnp.bfloat16)
    d_attended = jnp.dot(cotangent, proj_weight.T, preferred_element_type=jnp.float32).astype(jnp.bfloat16)
    head_outs, query_grads, key_grads, value_grads = lax.map(head_pass, (split_heads(query_pooled, N_TILE), split_heads(d_attended, N_TILE), split_heads(key_pooled, 1)[:, 0], split_heads(value_pooled, 1)[:, 0]))
    attended = join_heads(head_outs)
    pooled_input = mean_pool(tokens).astype(jnp.bfloat16)
    block_out = (jnp.dot(attended, proj_weight, preferred_element_type=jnp.float32) + jnp.dot(pooled_input, skip_weight.T, preferred_element_type=jnp.float32)).astype(jnp.bfloat16)
    proj_grad = jnp.dot(attended.T, cotangent, preferred_element_type=jnp.float32)
    d_pooled = jnp.dot(cotangent, skip_weight, preferred_element_type=jnp.float32)
    d_projected = jnp.stack([spread_field(join_heads(query_grads), query_pool, 2), spread_field(join_heads(key_grads), key_pool, 4), spread_field(join_heads(value_grads), value_pool, 4)]).astype(jnp.bfloat16)
    qkv_grad = jnp.stack([jnp.dot(d_projected[which].T, normed, preferred_element_type=jnp.float32) for which in range(3)])
    d_normed = jnp.dot(d_projected[0], qkv_weight[0], preferred_element_type=jnp.float32)
    d_normed = d_normed + jnp.dot(d_projected[1], qkv_weight[1], preferred_element_type=jnp.float32)
    d_normed = d_normed + jnp.dot(d_projected[2], qkv_weight[2], preferred_element_type=jnp.float32)
    input_grad = (norm_back(d_normed, unit_rows, inv_std, ln_gain) + expand_rows(d_pooled) * 0.25).astype(jnp.bfloat16)
    return (block_out, input_grad, qkv_grad, proj_grad)
```

```python
import functools

import jax
import jax.numpy as jnp
from jax import lax
from jax.experimental import pallas as pl
from jax.experimental.pallas import tpu as pltpu
from jax.sharding import PartitionSpec as P

HEAD_DIM = 96
TILE_H = 8
TILE_W = 32
EPSILON = 1e-06
SLAB = TILE_H * TILE_W // 16
CELLS = SLAB * 4
MESH = pl.DeviceIdType.MESH
F32 = jnp.float32
BF16 = jnp.bfloat16


def mm(a, b, contract=(1, 0)):
    return lax.dot_general(
        a, b, (((contract[0],), (contract[1],)), ((), ())), preferred_element_type=F32
    )


def token_order(shape, dim):
    p = lax.broadcasted_iota(jnp.int32, shape, dim)
    slab, block = p >> 4, p & 15
    a, b = slab >> 2, slab & 3
    return ((block >> 3) * 4 + a) * TILE_W + (block & 7) * 4 + b


def cell_order(shape, dim):
    p = lax.broadcasted_iota(jnp.int32, shape, dim)
    slab, block = p >> 4, p & 15
    a, b = slab >> 1, slab & 1
    return ((block >> 3) * 2 + a) * (TILE_W // 2) + (block & 7) * 2 + b


def one_hot(order, size, transposed=False):
    shape = (size, size)
    dim = 1 if transposed else 0
    other = lax.broadcasted_iota(jnp.int32, shape, 1 - dim)
    return jnp.where(order(shape, dim) == other, 1.0, 0.0).astype(BF16)


def rows(start, size):
    return pl.ds(pl.multiple_of(start, 16), size)


def kernel(
    n,
    nh,
    share_a,
    share_b,
    tokens_ref,
    gain_ref,
    qkv_ref,
    qpool_ref,
    kpool_ref,
    vpool_ref,
    proj_ref,
    skip_ref,
    cot_ref,
    block_out_ref,
    input_grad_ref,
    qkv_grad_ref,
    proj_grad_ref,
    cot_all,
    kv_all,
    kvg_send,
    kvg_recv,
    dp_send,
    dp_recv,
    hp_send,
    hp_recv,
    ga_send,
    ga_recv,
    ga_out,
    gb_send,
    gb_recv,
    gb_out,
    dn_send,
    dn_recv,
    ig_all,
    unit_ref,
    inv_ref,
    tile_send,
    tile_recv,
    head_send,
    head_recv,
):
    me = lax.axis_index("tile")
    my_head = lax.axis_index("head")
    chans = qkv_ref.shape[1]
    wide = qkv_ref.shape[2]
    share_h = unit_ref.shape[0] // nh

    def at_tile(k):
        return (lax.rem(me + k, n), my_head)

    def at_head(k):
        return (me, lax.rem(my_head + k, nh))

    def send_tile(stage, k, src, dst, device):
        copy = pltpu.make_async_remote_copy(
            src_ref=src,
            dst_ref=dst,
            send_sem=tile_send.at[stage, k],
            recv_sem=tile_recv.at[stage, k],
            device_id=device,
            device_id_type=MESH,
        )
        copy.start()
        return copy

    def send_head(stage, k, src, dst, device):
        copy = pltpu.make_async_remote_copy(
            src_ref=src,
            dst_ref=dst,
            send_sem=head_send.at[stage, k],
            recv_sem=head_recv.at[stage, k],
            device_id=device,
            device_id_type=MESH,
        )
        copy.start()
        return copy

    started = []

    def arrived(copies):
        for copy in copies:
            copy.wait_recv()
        started.extend(copies)

    barrier = pltpu.get_barrier_semaphore()
    for k in range(1, n):
        pl.semaphore_signal(barrier, inc=1, device_id=at_tile(k), device_id_type=MESH)
    for k in range(1, nh):
        pl.semaphore_signal(barrier, inc=1, device_id=at_head(k), device_id_type=MESH)

    order = one_hot(token_order, TILE_H * TILE_W)
    tokens = mm(order, tokens_ref[...])
    center = tokens - jnp.mean(tokens, axis=-1, keepdims=True)
    inv_std = lax.rsqrt(jnp.mean(center * center, axis=-1, keepdims=True) + EPSILON)
    unit = center * inv_std
    unit_ref[...] = unit
    inv_ref[...] = jnp.broadcast_to(inv_std, inv_ref.shape)
    gain = gain_ref[...]
    normed = (unit * gain).astype(BF16)

    kpool = kpool_ref[...].astype(F32)
    vpool = vpool_ref[...].astype(F32)
    qpool = qpool_ref[...].astype(F32)

    def pool_block(field, pool):
        total = pool[0:1] * field[0:SLAB]
        for s in range(1, 16):
            total = total + pool[s : s + 1] * field[s * SLAB : (s + 1) * SLAB]
        return total

    kv_all[0, 0:SLAB, :] = pool_block(mm(normed, qkv_ref[1], (1, 1)), kpool).astype(BF16)
    kv_all[1, 0:SLAB, :] = pool_block(mm(normed, qkv_ref[2], (1, 1)), vpool).astype(BF16)

    pl.semaphore_wait(barrier, n + nh - 2)
    kv_copies = [
        send_tile(
            0,
            k,
            kv_all.at[:, 0:SLAB],
            kv_all.at[:, k * SLAB : (k + 1) * SLAB],
            at_tile(k),
        )
        for k in range(1, n)
    ]
    cot_copies = [
        send_head(0, k, cot_ref, cot_all.at[my_head], at_head(k)) for k in range(1, nh)
    ]
    cot_all[my_head] = cot_ref[...]

    def cell_slabs(a, b):
        return [
            (2 * a2 + b2, (2 * a + a2) * 4 + 2 * b + b2) for a2 in range(2) for b2 in range(2)
        ]

    field = mm(normed, qkv_ref[0], (1, 1))
    query_parts = []
    input_parts = []
    for a in range(2):
        for b in range(2):
            total = None
            whole = None
            for w, s in cell_slabs(a, b):
                term = qpool[w : w + 1] * field[s * SLAB : (s + 1) * SLAB]
                total = term if total is None else total + term
                piece = tokens[s * SLAB : (s + 1) * SLAB]
                whole = piece if whole is None else whole + piece
            query_parts.append(total)
            input_parts.append(whole)
    queries_wide = jnp.concatenate(query_parts, axis=0).astype(BF16).astype(F32)
    pooled_input = (jnp.concatenate(input_parts, axis=0) * 0.25).astype(BF16)

    cells = one_hot(cell_order, CELLS)
    cells_back = one_hot(cell_order, CELLS, transposed=True)
    pooled_input = mm(cells_back, pooled_input).astype(BF16)
    skipped = mm(pooled_input, skip_ref[...], (1, 1))

    own_cot = mm(cells, cot_ref[...]).astype(BF16)
    d_pooled = mm(own_cot, skip_ref[...]).astype(BF16)
    half = CELLS // 2
    dp_send[0] = d_pooled[:half]
    dp_send[1] = d_pooled[half:]
    dp_copies = [
        send_head(
            1,
            k,
            dp_send.at[lax.rem(my_head + k, nh) * 2 // nh],
            dp_recv.at[k],
            at_head(k),
        )
        for k in range(1, nh)
    ]

    arrived(cot_copies)
    full_cot = jnp.concatenate([cot_all[h] for h in range(nh)], axis=1)
    full_cot = mm(cells, full_cot).astype(BF16)
    d_attended = mm(full_cot, proj_ref[...], (1, 1)).astype(BF16).astype(F32)

    heads = chans // HEAD_DIM
    lane = lax.broadcasted_iota(jnp.int32, (CELLS, chans), 1)
    masks = [
        jnp.logical_and(lane >= h * HEAD_DIM, lane < (h + 1) * HEAD_DIM) for h in range(heads)
    ]

    def by_head(x):
        return jnp.concatenate([jnp.where(m, x, 0.0) for m in masks], axis=0).astype(BF16)

    def from_heads(x):
        total = jnp.where(masks[0], x[:CELLS], 0.0)
        for h in range(1, heads):
            total = jnp.where(masks[h], x[h * CELLS : (h + 1) * CELLS], total)
        return total

    q_rows = by_head(queries_wide)
    g_rows = by_head(d_attended)

    arrived(kv_copies)
    keys = kv_all[0]
    values = kv_all[1]
    scale = HEAD_DIM ** (-0.5)
    exp_scores = jnp.exp(mm(q_rows, keys, (1, 1)) * scale)
    row_total = jnp.sum(exp_scores, axis=-1, keepdims=True)
    probs = (exp_scores / row_total).astype(BF16)
    dprobs = mm(g_rows, values, (1, 1))
    probs_wide = probs.astype(F32)
    row_delta = jnp.sum(probs_wide * dprobs, axis=-1, keepdims=True)
    d_scores = (scale * probs_wide * (dprobs - row_delta)).astype(BF16)
    key_grad = mm(d_scores, q_rows, (0, 0))
    value_grad = mm(probs, g_rows, (0, 0))
    kvg_send[0] = key_grad.astype(BF16)
    kvg_send[1] = value_grad.astype(BF16)
    kvg_copies = [
        send_tile(
            1,
            k,
            kvg_send.at[:, k * SLAB : (k + 1) * SLAB],
            kvg_recv.at[:, k * SLAB : (k + 1) * SLAB],
            at_tile(n - k),
        )
        for k in range(1, n)
    ]

    attended = (from_heads(mm(probs, values)) + queries_wide).astype(BF16)
    head_part = mm(mm(cells_back, attended).astype(BF16), proj_ref[...])
    for h in range(nh):
        hp_send[h] = head_part[:, h * chans : (h + 1) * chans].astype(BF16)
    hp_copies = [
        send_head(2, k, hp_send.at[lax.rem(my_head + k, nh)], hp_recv.at[k], at_head(k))
        for k in range(1, nh)
    ]

    query_grad = from_heads(mm(d_scores, keys)) + d_attended
    spread = []
    for s in range(16):
        a, b = s // 4, s % 4
        cell = (a // 2) * 2 + b // 2
        w = (a % 2) * 2 + b % 2
        spread.append(qpool[w : w + 1] * query_grad[cell * SLAB : (cell + 1) * SLAB])
    d_projected = jnp.concatenate(spread, axis=0).astype(BF16)
    ga_send[0:chans, :] = mm(d_projected, normed, (0, 0)).astype(BF16)
    proj_part = mm(attended, full_cot, (0, 0)).astype(BF16)
    halves = proj_part.shape[1] // wide
    for i in range(halves):
        ga_send[(i + 1) * chans : (i + 2) * chans, :] = proj_part[:, i * wide : (i + 1) * wide]
    filled = (halves + 1) * chans
    if ga_send.shape[0] > filled:
        ga_send[filled:, :] = jnp.zeros((ga_send.shape[0] - filled, wide), BF16)
    ga_copies = [
        send_tile(
            2,
            k,
            ga_send.at[rows(lax.rem(me + k, n) * share_a, share_a)],
            ga_recv.at[k],
            at_tile(k),
        )
        for k in range(1, n)
    ]
    d_normed = mm(d_projected, qkv_ref[0])

    arrived(kvg_copies)
    for j, pool, own in ((0, kpool, key_grad), (1, vpool, value_grad)):
        total = own[0:SLAB]
        for k in range(1, n):
            total = total + kvg_recv[j, k * SLAB : (k + 1) * SLAB, :].astype(F32)
        d_projected = jnp.concatenate([pool[s : s + 1] * total for s in range(16)], axis=0)
        d_projected = d_projected.astype(BF16)
        gb_send[j * chans : (j + 1) * chans, :] = mm(d_projected, normed, (0, 0)).astype(BF16)
        d_normed = d_normed + mm(d_projected, qkv_ref[j + 1])
    filled = 2 * chans
    if gb_send.shape[0] > filled:
        gb_send[filled:, :] = jnp.zeros((gb_send.shape[0] - filled, wide), BF16)
    gb_copies = [
        send_tile(
            3,
            k,
            gb_send.at[rows(lax.rem(me + k, n) * share_b, share_b)],
            gb_recv.at[k],
            at_tile(k),
        )
        for k in range(1, n)
    ]
    dn_send[...] = d_normed.astype(BF16)
    dn_copies = [
        send_head(
            3,
            k,
            dn_send.at[rows(lax.rem(my_head + k, nh) * share_h, share_h)],
            dn_recv.at[k],
            at_head(k),
        )
        for k in range(1, nh)
    ]

    def reduce_and_share(stage, copies, sent, received, out, share):
        arrived(copies)
        mine = rows(me * share, share)
        total = sent[mine, :].astype(F32)
        for k in range(1, n):
            total = total + received[k].astype(F32)
        out[mine, :] = total.astype(BF16)
        return [
            send_tile(stage, k, out.at[mine], out.at[mine], at_tile(k)) for k in range(1, n)
        ]

    ga_copies = reduce_and_share(4, ga_copies, ga_send, ga_recv, ga_out, share_a)

    arrived(hp_copies)
    summed = hp_send[my_head].astype(F32)
    for k in range(1, nh):
        summed = summed + hp_recv[k].astype(F32)
    block_out_ref[...] = (summed + skipped).astype(BF16)

    arrived(dp_copies)
    d_pooled = dp_send[my_head * 2 // nh].astype(F32)
    for k in range(1, nh):
        d_pooled = d_pooled + dp_recv[k].astype(F32)
    arrived(dn_copies)
    mine = rows(my_head * share_h, share_h)
    d_normed = dn_send[mine, :].astype(F32)
    for k in range(1, nh):
        d_normed = d_normed + dn_recv[k].astype(F32)
    scaled = d_normed * gain
    own_unit = unit_ref[mine, :]
    back = inv_ref[mine, :][:, 0:1] * (
        scaled
        - jnp.mean(scaled, axis=-1, keepdims=True)
        - own_unit * jnp.mean(scaled * own_unit, axis=-1, keepdims=True)
    )
    left, right = d_pooled[:SLAB], d_pooled[SLAB:]
    back = back + jnp.concatenate([left, left, right, right], axis=0) * 0.25
    ig_all[mine, :] = back.astype(BF16)
    ig_copies = [
        send_head(4, k, ig_all.at[mine], ig_all.at[mine], at_head(k)) for k in range(1, nh)
    ]

    gb_copies = reduce_and_share(5, gb_copies, gb_send, gb_recv, gb_out, share_b)

    arrived(ga_copies)
    qkv_grad_ref[0] = ga_out[0:chans, :]
    for i in range(halves):
        proj_grad_ref[:, i * wide : (i + 1) * wide] = ga_out[(i + 1) * chans : (i + 2) * chans, :]
    arrived(ig_copies)
    input_grad_ref[...] = mm(
        one_hot(token_order, TILE_H * TILE_W, transposed=True), ig_all[...]
    ).astype(BF16)
    arrived(gb_copies)
    qkv_grad_ref[1] = gb_out[0:chans, :]
    qkv_grad_ref[2] = gb_out[chans : 2 * chans, :]
    for copy in started:
        copy.wait_send()


def share_of(total, n):
    return -(-total // (n * 16)) * 16


def local(n, nh, *operands):
    tokens, ln_gain, qkv, qpool, kpool, vpool, proj, skip, cot = operands
    count, wide = tokens.shape
    chans = qkv.shape[1]
    full = proj.shape[1]
    share_a = share_of(chans * (1 + full // wide), n)
    share_b = share_of(chans * 2, n)
    share_h = count // nh
    vmem = pl.BlockSpec(memory_space=pltpu.VMEM)
    outs = pl.pallas_call(
        functools.partial(kernel, n, nh, share_a, share_b),
        out_shape=(
            jax.ShapeDtypeStruct(cot.shape, BF16),
            jax.ShapeDtypeStruct(tokens.shape, BF16),
            jax.ShapeDtypeStruct(qkv.shape, BF16),
            jax.ShapeDtypeStruct(proj.shape, BF16),
        ),
        in_specs=[vmem] * 9,
        out_specs=(vmem,) * 4,
        scratch_shapes=[
            pltpu.VMEM((nh,) + cot.shape, BF16),
            pltpu.VMEM((2, n * SLAB, chans), BF16),
            pltpu.VMEM((2, n * SLAB, chans), BF16),
            pltpu.VMEM((2, n * SLAB, chans), BF16),
            pltpu.VMEM((2, CELLS // 2, wide), BF16),
            pltpu.VMEM((nh, CELLS // 2, wide), BF16),
            pltpu.VMEM((nh,) + cot.shape, BF16),
            pltpu.VMEM((nh,) + cot.shape, BF16),
            pltpu.VMEM((n * share_a, wide), BF16),
            pltpu.VMEM((n, share_a, wide), BF16),
            pltpu.VMEM((n * share_a, wide), BF16),
            pltpu.VMEM((n * share_b, wide), BF16),
            pltpu.VMEM((n, share_b, wide), BF16),
            pltpu.VMEM((n * share_b, wide), BF16),
            pltpu.VMEM((count, wide), BF16),
            pltpu.VMEM((nh, share_h, wide), BF16),
            pltpu.VMEM((count, wide), BF16),
            pltpu.VMEM((count, wide), F32),
            pltpu.VMEM((count, 128), F32),
            pltpu.SemaphoreType.DMA((6, n)),
            pltpu.SemaphoreType.DMA((6, n)),
            pltpu.SemaphoreType.DMA((5, nh)),
            pltpu.SemaphoreType.DMA((5, nh)),
        ],
        compiler_params=pltpu.CompilerParams(
            collective_id=0, has_side_effects=True, vmem_limit_bytes=40 * 1024 * 1024
        ),
    )(tokens, ln_gain.reshape(1, -1), qkv, qpool, kpool, vpool, proj, skip, cot)
    block_out, input_grad, qkv_grad, proj_grad = outs
    return (block_out, input_grad, qkv_grad.astype(F32), proj_grad.astype(F32))


def solution(mesh):
    placed = (
        P("tile", None),
        P(),
        P(None, "head", None),
        P(None, "head"),
        P(None, "head"),
        P(None, "head"),
        P("head", None),
        P("head", None),
        P("tile", "head"),
    )
    return jax.shard_map(
        functools.partial(local, mesh.shape["tile"], mesh.shape["head"]),
        mesh=mesh,
        in_specs=placed,
        out_specs=(P("tile", "head"), P("tile", None), P(None, "head", None), P("head", None)),
        check_vma=False,
    )
```

```python
import functools

import jax
import jax.numpy as jnp
from jax import lax
from jax.experimental import pallas as pl
from jax.experimental.pallas import tpu as pltpu
from jax.sharding import PartitionSpec as P

HEAD_DIM = 96
TILE_H = 8
TILE_W = 32
EPSILON = 1e-06
SLAB = TILE_H * TILE_W // 16
CELLS = SLAB * 4
MESH = pl.DeviceIdType.MESH
F32 = jnp.float32
BF16 = jnp.bfloat16


def mm(a, b, contract=(1, 0)):
    return lax.dot_general(
        a, b, (((contract[0],), (contract[1],)), ((), ())), preferred_element_type=F32
    )


def token_order(shape, dim):
    p = lax.broadcasted_iota(jnp.int32, shape, dim)
    slab, block = p >> 4, p & 15
    a, b = slab >> 2, slab & 3
    return ((block >> 3) * 4 + a) * TILE_W + (block & 7) * 4 + b


def cell_order(shape, dim):
    p = lax.broadcasted_iota(jnp.int32, shape, dim)
    slab, block = p >> 4, p & 15
    a, b = slab >> 1, slab & 1
    return ((block >> 3) * 2 + a) * (TILE_W // 2) + (block & 7) * 2 + b


def one_hot(order, size, transposed=False):
    shape = (size, size)
    dim = 1 if transposed else 0
    other = lax.broadcasted_iota(jnp.int32, shape, 1 - dim)
    return jnp.where(order(shape, dim) == other, 1.0, 0.0).astype(BF16)


def rows(start, size):
    return pl.ds(pl.multiple_of(start, 16), size)


def kernel(
    n,
    nh,
    share_a,
    share_b,
    tokens_hbm,
    gain_hbm,
    qkv_hbm,
    qpool_hbm,
    kpool_hbm,
    vpool_hbm,
    proj_hbm,
    skip_hbm,
    cot_hbm,
    block_out_ref,
    ig_all,
    ga_out,
    gb_out,
    tokens_ref,
    gain_ref,
    qkv_ref,
    qpool_ref,
    kpool_ref,
    vpool_ref,
    proj_ref,
    skip_ref,
    cot_ref,
    cot_all,
    kv_all,
    kvg_send,
    kvg_recv,
    dp_send,
    dp_recv,
    hp_send,
    hp_recv,
    ga_send,
    ga_pair,
    ga_part,
    ga_recv,
    gb_send,
    gb_pair,
    gb_part,
    gb_recv,
    dn_send,
    dn_recv,
    unit_ref,
    inv_ref,
    load_sem,
    tile_send,
    tile_recv,
    head_send,
    head_recv,
):
    me = lax.axis_index("tile")
    my_head = lax.axis_index("head")
    chips = n // 2
    chip, core = me // 2, lax.rem(me, 2)
    chans = qkv_ref.shape[1]
    wide = qkv_ref.shape[2]
    share_h = unit_ref.shape[0] // nh

    def at_tile(k):
        return (lax.rem(me + k, n), my_head)

    def at_chip(k):
        return (lax.rem(chip + k, chips) * 2 + core, my_head)

    partner = (chip * 2 + 1 - core, my_head)

    def at_head(k):
        return (me, lax.rem(my_head + k, nh))

    def send_tile(stage, k, src, dst, device):
        copy = pltpu.make_async_remote_copy(
            src_ref=src,
            dst_ref=dst,
            send_sem=tile_send.at[stage, k],
            recv_sem=tile_recv.at[stage, k],
            device_id=device,
            device_id_type=MESH,
        )
        copy.start()
        return copy

    def send_head(stage, k, src, dst, device):
        copy = pltpu.make_async_remote_copy(
            src_ref=src,
            dst_ref=dst,
            send_sem=head_send.at[stage, k],
            recv_sem=head_recv.at[stage, k],
            device_id=device,
            device_id_type=MESH,
        )
        copy.start()
        return copy

    started = []

    def arrived(copies):
        for copy in copies:
            copy.wait_recv()
        started.extend(copies)

    barrier = pltpu.get_barrier_semaphore()
    for k in range(1, n):
        pl.semaphore_signal(barrier, inc=1, device_id=at_tile(k), device_id_type=MESH)
    for k in range(1, nh):
        pl.semaphore_signal(barrier, inc=1, device_id=at_head(k), device_id_type=MESH)

    loads = {}
    for i, (name, src, dst) in enumerate(
        (
            ("tokens", tokens_hbm, tokens_ref),
            ("gain", gain_hbm, gain_ref),
            ("qkv", qkv_hbm, qkv_ref),
            ("kpool", kpool_hbm, kpool_ref),
            ("vpool", vpool_hbm, vpool_ref),
            ("cot", cot_hbm, cot_ref),
            ("qpool", qpool_hbm, qpool_ref),
            ("skip", skip_hbm, skip_ref),
            ("proj", proj_hbm, proj_ref),
        )
    ):
        loads[name] = pltpu.make_async_copy(src, dst, load_sem.at[i])
        loads[name].start()

    order = one_hot(token_order, TILE_H * TILE_W)
    loads["tokens"].wait()
    tokens = mm(order, tokens_ref[...])
    center = tokens - jnp.mean(tokens, axis=-1, keepdims=True)
    inv_std = lax.rsqrt(jnp.mean(center * center, axis=-1, keepdims=True) + EPSILON)
    unit = center * inv_std
    unit_ref[...] = unit
    inv_ref[...] = jnp.broadcast_to(inv_std, inv_ref.shape)
    loads["gain"].wait()
    gain = gain_ref[...].reshape(1, wide)
    normed = (unit * gain).astype(BF16)

    for name in ("qkv", "kpool", "vpool", "cot", "qpool"):
        loads[name].wait()
    kpool = kpool_ref[...].astype(F32)
    vpool = vpool_ref[...].astype(F32)
    qpool = qpool_ref[...].astype(F32)

    def pool_block(field, pool):
        total = pool[0:1] * field[0:SLAB]
        for s in range(1, 16):
            total = total + pool[s : s + 1] * field[s * SLAB : (s + 1) * SLAB]
        return total

    kv_all[0, 0:SLAB, :] = pool_block(mm(normed, qkv_ref[1], (1, 1)), kpool).astype(BF16)
    kv_all[1, 0:SLAB, :] = pool_block(mm(normed, qkv_ref[2], (1, 1)), vpool).astype(BF16)

    pl.semaphore_wait(barrier, n + nh - 2)
    kv_copies = [
        send_tile(
            0,
            k,
            kv_all.at[:, 0:SLAB],
            kv_all.at[:, k * SLAB : (k + 1) * SLAB],
            at_tile(k),
        )
        for k in range(1, n)
    ]
    cot_copies = [
        send_head(0, k, cot_ref, cot_all.at[my_head], at_head(k)) for k in range(1, nh)
    ]
    cot_all[my_head] = cot_ref[...]

    def cell_slabs(a, b):
        return [
            (2 * a2 + b2, (2 * a + a2) * 4 + 2 * b + b2) for a2 in range(2) for b2 in range(2)
        ]

    field = mm(normed, qkv_ref[0], (1, 1))
    query_parts = []
    input_parts = []
    for a in range(2):
        for b in range(2):
            total = None
            whole = None
            for w, s in cell_slabs(a, b):
                term = qpool[w : w + 1] * field[s * SLAB : (s + 1) * SLAB]
                total = term if total is None else total + term
                piece = tokens[s * SLAB : (s + 1) * SLAB]
                whole = piece if whole is None else whole + piece
            query_parts.append(total)
            input_parts.append(whole)
    queries_wide = jnp.concatenate(query_parts, axis=0).astype(BF16).astype(F32)
    pooled_input = (jnp.concatenate(input_parts, axis=0) * 0.25).astype(BF16)

    cells = one_hot(cell_order, CELLS)
    cells_back = one_hot(cell_order, CELLS, transposed=True)
    pooled_input = mm(cells_back, pooled_input).astype(BF16)
    loads["skip"].wait()
    skipped = mm(pooled_input, skip_ref[...], (1, 1))

    own_cot = mm(cells, cot_ref[...]).astype(BF16)
    d_pooled = mm(own_cot, skip_ref[...]).astype(BF16)
    half = CELLS // 2
    dp_send[0] = d_pooled[:half]
    dp_send[1] = d_pooled[half:]
    dp_copies = [
        send_head(
            1,
            k,
            dp_send.at[lax.rem(my_head + k, nh) * 2 // nh],
            dp_recv.at[k],
            at_head(k),
        )
        for k in range(1, nh)
    ]

    loads["proj"].wait()
    arrived(cot_copies)
    full_cot = jnp.concatenate([cot_all[h] for h in range(nh)], axis=1)
    full_cot = mm(cells, full_cot).astype(BF16)
    d_attended = mm(full_cot, proj_ref[...], (1, 1)).astype(BF16).astype(F32)

    heads = chans // HEAD_DIM
    lane = lax.broadcasted_iota(jnp.int32, (CELLS, chans), 1)
    masks = [
        jnp.logical_and(lane >= h * HEAD_DIM, lane < (h + 1) * HEAD_DIM) for h in range(heads)
    ]

    def by_head(x):
        return jnp.concatenate([jnp.where(m, x, 0.0) for m in masks], axis=0).astype(BF16)

    def from_heads(x):
        total = jnp.where(masks[0], x[:CELLS], 0.0)
        for h in range(1, heads):
            total = jnp.where(masks[h], x[h * CELLS : (h + 1) * CELLS], total)
        return total

    q_rows = by_head(queries_wide)
    g_rows = by_head(d_attended)

    arrived(kv_copies)
    keys = kv_all[0]
    values = kv_all[1]
    scale = HEAD_DIM ** (-0.5)
    exp_scores = jnp.exp(mm(q_rows, keys, (1, 1)) * scale)
    row_total = jnp.sum(exp_scores, axis=-1, keepdims=True)
    probs = (exp_scores / row_total).astype(BF16)
    dprobs = mm(g_rows, values, (1, 1))
    probs_wide = probs.astype(F32)
    row_delta = jnp.sum(probs_wide * dprobs, axis=-1, keepdims=True)
    d_scores = (scale * probs_wide * (dprobs - row_delta)).astype(BF16)
    key_grad = mm(d_scores, q_rows, (0, 0))
    value_grad = mm(probs, g_rows, (0, 0))
    kvg_send[0] = key_grad.astype(BF16)
    kvg_send[1] = value_grad.astype(BF16)
    kvg_copies = [
        send_tile(
            1,
            k,
            kvg_send.at[:, k * SLAB : (k + 1) * SLAB],
            kvg_recv.at[:, k * SLAB : (k + 1) * SLAB],
            at_tile(n - k),
        )
        for k in range(1, n)
    ]

    attended = (from_heads(mm(probs, values)) + queries_wide).astype(BF16)
    head_part = mm(mm(cells_back, attended).astype(BF16), proj_ref[...])
    for h in range(nh):
        hp_send[h] = head_part[:, h * chans : (h + 1) * chans].astype(BF16)
    hp_copies = [
        send_head(2, k, hp_send.at[lax.rem(my_head + k, nh)], hp_recv.at[k], at_head(k))
        for k in range(1, nh)
    ]

    query_grad = from_heads(mm(d_scores, keys)) + d_attended
    spread = []
    for s in range(16):
        a, b = s // 4, s % 4
        cell = (a // 2) * 2 + b // 2
        w = (a % 2) * 2 + b % 2
        spread.append(qpool[w : w + 1] * query_grad[cell * SLAB : (cell + 1) * SLAB])
    d_projected = jnp.concatenate(spread, axis=0).astype(BF16)
    ga_send[0:chans, :] = mm(d_projected, normed, (0, 0)).astype(BF16)
    proj_part = mm(attended, full_cot, (0, 0)).astype(BF16)
    halves = proj_part.shape[1] // wide
    for i in range(halves):
        ga_send[(i + 1) * chans : (i + 2) * chans, :] = proj_part[:, i * wide : (i + 1) * wide]
    filled = (halves + 1) * chans
    if ga_send.shape[0] > filled:
        ga_send[filled:, :] = jnp.zeros((ga_send.shape[0] - filled, wide), BF16)
    half_a, half_b = chips * share_a, chips * share_b
    ga_pairs = [
        send_tile(2, 1, ga_send.at[rows((1 - core) * half_a, half_a)], ga_pair, partner)
    ]
    d_normed = mm(d_projected, qkv_ref[0])

    arrived(kvg_copies)
    d_fields = []
    for j, pool, own in ((0, kpool, key_grad), (1, vpool, value_grad)):
        total = own[0:SLAB]
        for k in range(1, n):
            total = total + kvg_recv[j, k * SLAB : (k + 1) * SLAB, :].astype(F32)
        d_projected = jnp.concatenate([pool[s : s + 1] * total for s in range(16)], axis=0)
        d_fields.append(d_projected.astype(BF16))
        d_normed = d_normed + mm(d_fields[j], qkv_ref[j + 1])
    dn_send[...] = d_normed.astype(BF16)
    dn_copies = [
        send_head(
            3,
            k,
            dn_send.at[rows(lax.rem(my_head + k, nh) * share_h, share_h)],
            dn_recv.at[k],
            at_head(k),
        )
        for k in range(1, nh)
    ]
    for j in range(2):
        gb_send[j * chans : (j + 1) * chans, :] = mm(d_fields[j], normed, (0, 0)).astype(BF16)
    filled = 2 * chans
    if gb_send.shape[0] > filled:
        gb_send[filled:, :] = jnp.zeros((gb_send.shape[0] - filled, wide), BF16)
    gb_pairs = [
        send_tile(6, 1, gb_send.at[rows((1 - core) * half_b, half_b)], gb_pair, partner)
    ]

    def fold(stage, pairs, sent, pair, part, received, share):
        arrived(pairs)
        size = chips * share
        total = sent[rows(core * size, size), :].astype(F32) + pair[...].astype(F32)
        part[...] = total.astype(BF16)
        return [
            send_tile(
                stage,
                k,
                part.at[rows(lax.rem(chip + k, chips) * share, share)],
                received.at[k],
                at_chip(k),
            )
            for k in range(1, chips)
        ]

    def place(k, share):
        from_chip = lax.rem(chip + chips - k, chips)
        return rows((core * chips + from_chip) * share, share)

    def reduce_and_share(stage, copies, part, received, out, share):
        arrived(copies)
        total = part[rows(chip * share, share), :].astype(F32)
        for k in range(1, chips):
            total = total + received[k].astype(F32)
        mine = place(0, share)
        out[mine, :] = total.astype(BF16)
        shares = [
            send_tile(stage, k, out.at[mine], out.at[mine], at_chip(k))
            for k in range(1, chips)
        ]
        relays = [send_tile(stage + 1, 0, out.at[mine], out.at[mine], partner)]
        return shares, relays

    def relay(stage, shares, relays, out, share):
        for k in range(1, chips):
            arrived(shares[k - 1 : k])
            there = place(k, share)
            relays.append(send_tile(stage, k, out.at[there], out.at[there], partner))

    ga_copies = fold(3, ga_pairs, ga_send, ga_pair, ga_part, ga_recv, share_a)
    gb_copies = fold(7, gb_pairs, gb_send, gb_pair, gb_part, gb_recv, share_b)
    ga_shares, ga_relays = reduce_and_share(4, ga_copies, ga_part, ga_recv, ga_out, share_a)

    arrived(hp_copies)
    summed = hp_send[my_head].astype(F32)
    for k in range(1, nh):
        summed = summed + hp_recv[k].astype(F32)
    block_out_ref[...] = (summed + skipped).astype(BF16)

    arrived(dp_copies)
    d_pooled = dp_send[my_head * 2 // nh].astype(F32)
    for k in range(1, nh):
        d_pooled = d_pooled + dp_recv[k].astype(F32)
    arrived(dn_copies)
    mine = rows(my_head * share_h, share_h)
    d_normed = dn_send[mine, :].astype(F32)
    for k in range(1, nh):
        d_normed = d_normed + dn_recv[k].astype(F32)
    scaled = d_normed * gain
    own_unit = unit_ref[mine, :]
    back = inv_ref[mine, :][:, 0:1] * (
        scaled
        - jnp.mean(scaled, axis=-1, keepdims=True)
        - own_unit * jnp.mean(scaled * own_unit, axis=-1, keepdims=True)
    )
    left, right = d_pooled[:SLAB], d_pooled[SLAB:]
    back = back + jnp.concatenate([left, left, right, right], axis=0) * 0.25
    ig_all[mine, :] = back.astype(BF16)
    ig_copies = [
        send_head(4, k, ig_all.at[mine], ig_all.at[mine], at_head(k)) for k in range(1, nh)
    ]

    gb_shares, gb_relays = reduce_and_share(8, gb_copies, gb_part, gb_recv, gb_out, share_b)
    relay(5, ga_shares, ga_relays, ga_out, share_a)
    relay(9, gb_shares, gb_relays, gb_out, share_b)
    arrived(ig_copies)
    arrived(ga_relays)
    arrived(gb_relays)
    for copy in started:
        copy.wait_send()


def finish(
    block_ref, ig_ref, ga_ref, gb_ref, block_hbm, ig_hbm, qkv_hbm, proj_hbm, ig, qkv, proj, sems
):
    chans, wide = qkv.shape[1:]
    copies = [pltpu.make_async_copy(block_ref, block_hbm, sems.at[0])]
    copies[0].start()

    def put(src, dst):
        copy = pltpu.make_async_copy(src, dst, sems.at[len(copies)])
        copy.start()
        copies.append(copy)

    for i in range(proj.shape[1] // wide):
        proj[:, i * wide : (i + 1) * wide] = ga_ref[
            (i + 1) * chans : (i + 2) * chans, :
        ].astype(F32)
    put(proj, proj_hbm)
    for j, part in enumerate(
        (ga_ref[0:chans, :], gb_ref[0:chans, :], gb_ref[chans : 2 * chans, :])
    ):
        qkv[j] = part.astype(F32)
        put(qkv.at[j], qkv_hbm.at[j])
    back = one_hot(token_order, TILE_H * TILE_W, transposed=True)
    ig[...] = mm(back, ig_ref[...]).astype(BF16)
    put(ig, ig_hbm)
    for copy in copies:
        copy.wait()


def share_of(total, n):
    return -(-total // (n * 16)) * 16


def local(n, nh, *operands):
    tokens, ln_gain, qkv, qpool, kpool, vpool, proj, skip, cot = operands
    count, wide = tokens.shape
    chans = qkv.shape[1]
    full = proj.shape[1]
    share_a = share_of(chans * (1 + full // wide), n)
    share_b = share_of(chans * 2, n)
    share_h = count // nh
    vmem = pl.BlockSpec(memory_space=pltpu.VMEM)
    hbm = pl.BlockSpec(memory_space=pltpu.HBM)
    outs = pl.pallas_call(
        functools.partial(kernel, n, nh, share_a, share_b),
        out_shape=(
            jax.ShapeDtypeStruct(cot.shape, BF16),
            jax.ShapeDtypeStruct(tokens.shape, BF16),
            jax.ShapeDtypeStruct((n * share_a, wide), BF16),
            jax.ShapeDtypeStruct((n * share_b, wide), BF16),
        ),
        in_specs=[hbm] * 9,
        out_specs=(vmem,) * 4,
        scratch_shapes=[pltpu.VMEM(x.shape, x.dtype) for x in operands]
        + [
            pltpu.VMEM((nh,) + cot.shape, BF16),
            pltpu.VMEM((2, n * SLAB, chans), BF16),
            pltpu.VMEM((2, n * SLAB, chans), BF16),
            pltpu.VMEM((2, n * SLAB, chans), BF16),
            pltpu.VMEM((2, CELLS // 2, wide), BF16),
            pltpu.VMEM((nh, CELLS // 2, wide), BF16),
            pltpu.VMEM((nh,) + cot.shape, BF16),
            pltpu.VMEM((nh,) + cot.shape, BF16),
            pltpu.VMEM((n * share_a, wide), BF16),
            pltpu.VMEM((n // 2 * share_a, wide), BF16),
            pltpu.VMEM((n // 2 * share_a, wide), BF16),
            pltpu.VMEM((n // 2, share_a, wide), BF16),
            pltpu.VMEM((n * share_b, wide), BF16),
            pltpu.VMEM((n // 2 * share_b, wide), BF16),
            pltpu.VMEM((n // 2 * share_b, wide), BF16),
            pltpu.VMEM((n // 2, share_b, wide), BF16),
            pltpu.VMEM((count, wide), BF16),
            pltpu.VMEM((nh, share_h, wide), BF16),
            pltpu.VMEM((count, wide), F32),
            pltpu.VMEM((count, 128), F32),
            pltpu.SemaphoreType.DMA((9,)),
            pltpu.SemaphoreType.DMA((10, n)),
            pltpu.SemaphoreType.DMA((10, n)),
            pltpu.SemaphoreType.DMA((5, nh)),
            pltpu.SemaphoreType.DMA((5, nh)),
        ],
        compiler_params=pltpu.CompilerParams(
            collective_id=0, has_side_effects=True, vmem_limit_bytes=40 * 1024 * 1024
        ),
    )(*[pltpu.with_memory_space_constraint(x, pltpu.HBM) for x in operands])
    return pl.pallas_call(
        finish,
        out_shape=(
            jax.ShapeDtypeStruct(cot.shape, BF16),
            jax.ShapeDtypeStruct(tokens.shape, BF16),
            jax.ShapeDtypeStruct(qkv.shape, F32),
            jax.ShapeDtypeStruct(proj.shape, F32),
        ),
        in_specs=[vmem] * 4,
        out_specs=(hbm,) * 4,
        scratch_shapes=[
            pltpu.VMEM(tokens.shape, BF16),
            pltpu.VMEM(qkv.shape, F32),
            pltpu.VMEM(proj.shape, F32),
            pltpu.SemaphoreType.DMA((6,)),
        ],
        compiler_params=pltpu.CompilerParams(vmem_limit_bytes=16 * 1024 * 1024),
    )(*outs)


def solution(mesh):
    placed = (
        P("tile", None),
        P(),
        P(None, "head", None),
        P(None, "head"),
        P(None, "head"),
        P(None, "head"),
        P("head", None),
        P("head", None),
        P("tile", "head"),
    )
    return jax.shard_map(
        functools.partial(local, mesh.shape["tile"], mesh.shape["head"]),
        mesh=mesh,
        in_specs=placed,
        out_specs=(P("tile", "head"), P("tile", None), P(None, "head", None), P("head", None)),
        check_vma=False,
    )
```

```python
import functools

import jax
import jax.numpy as jnp
from jax import lax
from jax.experimental import pallas as pl
from jax.experimental.pallas import tpu as pltpu
from jax.sharding import PartitionSpec as P

HEAD_DIM = 96
TILE_H = 8
TILE_W = 32
EPSILON = 1e-06
SLAB = TILE_H * TILE_W // 16
CELLS = SLAB * 4
MESH = pl.DeviceIdType.MESH
F32 = jnp.float32
BF16 = jnp.bfloat16


def mm(a, b, contract=(1, 0)):
    return lax.dot_general(
        a, b, (((contract[0],), (contract[1],)), ((), ())), preferred_element_type=F32
    )


def token_order(shape, dim):
    p = lax.broadcasted_iota(jnp.int32, shape, dim)
    slab, block = p >> 4, p & 15
    a, b = slab >> 2, slab & 3
    return ((block >> 3) * 4 + a) * TILE_W + (block & 7) * 4 + b


def cell_order(shape, dim):
    p = lax.broadcasted_iota(jnp.int32, shape, dim)
    slab, block = p >> 4, p & 15
    a, b = slab >> 1, slab & 1
    return ((block >> 3) * 2 + a) * (TILE_W // 2) + (block & 7) * 2 + b


def one_hot(order, size, transposed=False):
    shape = (size, size)
    dim = 1 if transposed else 0
    other = lax.broadcasted_iota(jnp.int32, shape, 1 - dim)
    return jnp.where(order(shape, dim) == other, 1.0, 0.0).astype(BF16)


def rows(start, size):
    return pl.ds(pl.multiple_of(start, 16), size)


def kernel(
    n,
    nh,
    share_a,
    share_b,
    tokens_hbm,
    gain_hbm,
    qkv_hbm,
    qpool_hbm,
    kpool_hbm,
    vpool_hbm,
    proj_hbm,
    skip_hbm,
    cot_hbm,
    block_out_ref,
    ig_all,
    ga_out,
    gb_out,
    tokens_ref,
    gain_ref,
    qkv_ref,
    qpool_ref,
    kpool_ref,
    vpool_ref,
    proj_ref,
    skip_ref,
    cot_ref,
    cot_all,
    kv_all,
    kvg_send,
    kvg_recv,
    dp_send,
    dp_recv,
    hp_send,
    hp_recv,
    ga_send,
    ga_pair,
    ga_part,
    ga_recv,
    gb_send,
    gb_pair,
    gb_part,
    gb_recv,
    dn_send,
    dn_recv,
    unit_ref,
    inv_ref,
    load_sem,
    tile_send,
    tile_recv,
    head_send,
    head_recv,
):
    me = lax.axis_index("tile")
    my_head = lax.axis_index("head")
    chips = n // 2
    chip, core = me // 2, lax.rem(me, 2)
    chans = qkv_ref.shape[1]
    wide = qkv_ref.shape[2]
    share_h = unit_ref.shape[0] // nh

    def at_tile(k):
        return (lax.rem(me + k, n), my_head)

    def at_chip(k):
        return (lax.rem(chip + k, chips) * 2 + core, my_head)

    partner = (chip * 2 + 1 - core, my_head)

    def at_head(k):
        return (me, lax.rem(my_head + k, nh))

    def send_tile(stage, k, src, dst, device):
        copy = pltpu.make_async_remote_copy(
            src_ref=src,
            dst_ref=dst,
            send_sem=tile_send.at[stage, k],
            recv_sem=tile_recv.at[stage, k],
            device_id=device,
            device_id_type=MESH,
        )
        copy.start()
        return copy

    def send_head(stage, k, src, dst, device):
        copy = pltpu.make_async_remote_copy(
            src_ref=src,
            dst_ref=dst,
            send_sem=head_send.at[stage, k],
            recv_sem=head_recv.at[stage, k],
            device_id=device,
            device_id_type=MESH,
        )
        copy.start()
        return copy

    started = []

    def arrived(copies):
        for copy in copies:
            copy.wait_recv()
        started.extend(copies)

    barrier = pltpu.get_barrier_semaphore()
    for k in range(1, n):
        pl.semaphore_signal(barrier, inc=1, device_id=at_tile(k), device_id_type=MESH)
    for k in range(1, nh):
        pl.semaphore_signal(barrier, inc=1, device_id=at_head(k), device_id_type=MESH)

    loads = {}
    for i, (name, src, dst) in enumerate(
        (
            ("cot", cot_hbm, cot_ref),
            ("tokens", tokens_hbm, tokens_ref),
            ("gain", gain_hbm, gain_ref),
            ("qkv", qkv_hbm, qkv_ref),
            ("kpool", kpool_hbm, kpool_ref),
            ("vpool", vpool_hbm, vpool_ref),
            ("qpool", qpool_hbm, qpool_ref),
            ("skip", skip_hbm, skip_ref),
            ("proj", proj_hbm, proj_ref),
        )
    ):
        loads[name] = pltpu.make_async_copy(src, dst, load_sem.at[i])
        loads[name].start()

    loads["cot"].wait()
    cot_all[my_head] = cot_ref[...]
    pl.semaphore_wait(barrier, n + nh - 2)
    cot_copies = [
        send_head(0, k, cot_ref, cot_all.at[my_head], at_head(k)) for k in range(1, nh)
    ]

    order = one_hot(token_order, TILE_H * TILE_W)
    loads["tokens"].wait()
    tokens = mm(order, tokens_ref[...])
    center = tokens - jnp.mean(tokens, axis=-1, keepdims=True)
    inv_std = lax.rsqrt(jnp.mean(center * center, axis=-1, keepdims=True) + EPSILON)
    unit = center * inv_std
    unit_ref[...] = unit
    inv_ref[...] = jnp.broadcast_to(inv_std, inv_ref.shape)
    loads["gain"].wait()
    gain = gain_ref[...].reshape(1, wide)
    normed = (unit * gain).astype(BF16)

    for name in ("qkv", "kpool", "vpool"):
        loads[name].wait()
    kpool = kpool_ref[...].astype(F32)
    vpool = vpool_ref[...].astype(F32)

    def pool_block(field, pool):
        total = pool[0:1] * field[0:SLAB]
        for s in range(1, 16):
            total = total + pool[s : s + 1] * field[s * SLAB : (s + 1) * SLAB]
        return total

    kv_all[0, 0:SLAB, :] = pool_block(mm(normed, qkv_ref[1], (1, 1)), kpool).astype(BF16)
    kv_all[1, 0:SLAB, :] = pool_block(mm(normed, qkv_ref[2], (1, 1)), vpool).astype(BF16)

    kv_copies = [
        send_tile(
            0,
            k,
            kv_all.at[:, 0:SLAB],
            kv_all.at[:, k * SLAB : (k + 1) * SLAB],
            at_tile(k),
        )
        for k in range(1, n)
    ]

    def cell_slabs(a, b):
        return [
            (2 * a2 + b2, (2 * a + a2) * 4 + 2 * b + b2) for a2 in range(2) for b2 in range(2)
        ]

    loads["qpool"].wait()
    qpool = qpool_ref[...].astype(F32)
    field = mm(normed, qkv_ref[0], (1, 1))
    query_parts = []
    input_parts = []
    for a in range(2):
        for b in range(2):
            total = None
            whole = None
            for w, s in cell_slabs(a, b):
                term = qpool[w : w + 1] * field[s * SLAB : (s + 1) * SLAB]
                total = term if total is None else total + term
                piece = tokens[s * SLAB : (s + 1) * SLAB]
                whole = piece if whole is None else whole + piece
            query_parts.append(total)
            input_parts.append(whole)
    queries_wide = jnp.concatenate(query_parts, axis=0).astype(BF16).astype(F32)
    pooled_input = (jnp.concatenate(input_parts, axis=0) * 0.25).astype(BF16)

    cells = one_hot(cell_order, CELLS)
    cells_back = one_hot(cell_order, CELLS, transposed=True)
    loads["skip"].wait()

    own_cot = mm(cells, cot_ref[...]).astype(BF16)
    d_pooled = mm(own_cot, skip_ref[...]).astype(BF16)
    half = CELLS // 2
    dp_send[0] = d_pooled[:half]
    dp_send[1] = d_pooled[half:]
    dp_copies = [
        send_head(
            1,
            k,
            dp_send.at[lax.rem(my_head + k, nh) * 2 // nh],
            dp_recv.at[k],
            at_head(k),
        )
        for k in range(1, nh)
    ]

    loads["proj"].wait()
    arrived(cot_copies)
    full_cot = jnp.concatenate([cot_all[h] for h in range(nh)], axis=1)
    full_cot = mm(cells, full_cot).astype(BF16)
    d_attended = mm(full_cot, proj_ref[...], (1, 1)).astype(BF16).astype(F32)

    heads = chans // HEAD_DIM
    lane = lax.broadcasted_iota(jnp.int32, (CELLS, chans), 1)
    masks = [
        jnp.logical_and(lane >= h * HEAD_DIM, lane < (h + 1) * HEAD_DIM) for h in range(heads)
    ]

    def by_head(x):
        return jnp.concatenate([jnp.where(m, x, 0.0) for m in masks], axis=0).astype(BF16)

    def from_heads(x):
        total = jnp.where(masks[0], x[:CELLS], 0.0)
        for h in range(1, heads):
            total = jnp.where(masks[h], x[h * CELLS : (h + 1) * CELLS], total)
        return total

    q_rows = by_head(queries_wide)
    g_rows = by_head(d_attended)

    arrived(kv_copies)
    keys = kv_all[0]
    values = kv_all[1]
    scale = HEAD_DIM ** (-0.5)
    exp_scores = jnp.exp(mm(q_rows, keys, (1, 1)) * scale)
    row_total = jnp.sum(exp_scores, axis=-1, keepdims=True)
    probs = (exp_scores / row_total).astype(BF16)
    dprobs = mm(g_rows, values, (1, 1))
    probs_wide = probs.astype(F32)
    row_delta = jnp.sum(probs_wide * dprobs, axis=-1, keepdims=True)
    d_scores = (scale * probs_wide * (dprobs - row_delta)).astype(BF16)
    key_grad = mm(d_scores, q_rows, (0, 0))
    value_grad = mm(probs, g_rows, (0, 0))
    kvg_send[0] = key_grad.astype(BF16)
    kvg_send[1] = value_grad.astype(BF16)
    kvg_copies = [
        send_tile(
            1,
            k,
            kvg_send.at[:, k * SLAB : (k + 1) * SLAB],
            kvg_recv.at[:, k * SLAB : (k + 1) * SLAB],
            at_tile(n - k),
        )
        for k in range(1, n)
    ]

    attended = (from_heads(mm(probs, values)) + queries_wide).astype(BF16)
    head_part = mm(mm(cells_back, attended).astype(BF16), proj_ref[...])
    for h in range(nh):
        hp_send[h] = head_part[:, h * chans : (h + 1) * chans].astype(BF16)
    hp_copies = [
        send_head(2, k, hp_send.at[lax.rem(my_head + k, nh)], hp_recv.at[k], at_head(k))
        for k in range(1, nh)
    ]

    query_grad = from_heads(mm(d_scores, keys)) + d_attended
    spread = []
    for s in range(16):
        a, b = s // 4, s % 4
        cell = (a // 2) * 2 + b // 2
        w = (a % 2) * 2 + b % 2
        spread.append(qpool[w : w + 1] * query_grad[cell * SLAB : (cell + 1) * SLAB])
    d_projected = jnp.concatenate(spread, axis=0).astype(BF16)
    ga_send[0:chans, :] = mm(d_projected, normed, (0, 0)).astype(BF16)
    proj_part = mm(attended, full_cot, (0, 0)).astype(BF16)
    halves = proj_part.shape[1] // wide
    for i in range(halves):
        ga_send[(i + 1) * chans : (i + 2) * chans, :] = proj_part[:, i * wide : (i + 1) * wide]
    filled = (halves + 1) * chans
    if ga_send.shape[0] > filled:
        ga_send[filled:, :] = jnp.zeros((ga_send.shape[0] - filled, wide), BF16)
    half_a, half_b = chips * share_a, chips * share_b
    ga_pairs = [
        send_tile(2, 1, ga_send.at[rows((1 - core) * half_a, half_a)], ga_pair, partner)
    ]
    d_normed = mm(d_projected, qkv_ref[0])

    def fold(stage, pairs, sent, pair, part, received, share):
        arrived(pairs)
        size = chips * share
        total = sent[rows(core * size, size), :].astype(F32) + pair[...].astype(F32)
        part[...] = total.astype(BF16)
        return [
            send_tile(
                stage,
                k,
                part.at[rows(lax.rem(chip + k, chips) * share, share)],
                received.at[k],
                at_chip(k),
            )
            for k in range(1, chips)
        ]

    def place(k, share):
        from_chip = lax.rem(chip + chips - k, chips)
        return rows((core * chips + from_chip) * share, share)

    def reduce_and_share(stage, copies, part, received, out, share):
        arrived(copies)
        total = part[rows(chip * share, share), :].astype(F32)
        for k in range(1, chips):
            total = total + received[k].astype(F32)
        mine = place(0, share)
        out[mine, :] = total.astype(BF16)
        shares = [
            send_tile(stage, k, out.at[mine], out.at[mine], at_chip(k))
            for k in range(1, chips)
        ]
        relays = [send_tile(stage + 1, 0, out.at[mine], out.at[mine], partner)]
        return shares, relays

    def relay(stage, shares, relays, out, share):
        for k in range(1, chips):
            arrived(shares[k - 1 : k])
            there = place(k, share)
            relays.append(send_tile(stage, k, out.at[there], out.at[there], partner))

    ga_copies = fold(3, ga_pairs, ga_send, ga_pair, ga_part, ga_recv, share_a)

    arrived(kvg_copies)
    d_fields = []
    for j, pool, own in ((0, kpool, key_grad), (1, vpool, value_grad)):
        total = own[0:SLAB]
        for k in range(1, n):
            total = total + kvg_recv[j, k * SLAB : (k + 1) * SLAB, :].astype(F32)
        d_projected = jnp.concatenate([pool[s : s + 1] * total for s in range(16)], axis=0)
        d_fields.append(d_projected.astype(BF16))
        d_normed = d_normed + mm(d_fields[j], qkv_ref[j + 1])
    dn_send[...] = d_normed.astype(BF16)
    dn_copies = [
        send_head(
            3,
            k,
            dn_send.at[rows(lax.rem(my_head + k, nh) * share_h, share_h)],
            dn_recv.at[k],
            at_head(k),
        )
        for k in range(1, nh)
    ]
    for j in range(2):
        gb_send[j * chans : (j + 1) * chans, :] = mm(d_fields[j], normed, (0, 0)).astype(BF16)
    filled = 2 * chans
    if gb_send.shape[0] > filled:
        gb_send[filled:, :] = jnp.zeros((gb_send.shape[0] - filled, wide), BF16)
    gb_pairs = [
        send_tile(6, 1, gb_send.at[rows((1 - core) * half_b, half_b)], gb_pair, partner)
    ]

    gb_copies = fold(7, gb_pairs, gb_send, gb_pair, gb_part, gb_recv, share_b)
    ga_shares, ga_relays = reduce_and_share(4, ga_copies, ga_part, ga_recv, ga_out, share_a)

    pooled_input = mm(cells_back, pooled_input).astype(BF16)
    skipped = mm(pooled_input, skip_ref[...], (1, 1))
    arrived(hp_copies)
    summed = hp_send[my_head].astype(F32)
    for k in range(1, nh):
        summed = summed + hp_recv[k].astype(F32)
    block_out_ref[...] = (summed + skipped).astype(BF16)

    arrived(dp_copies)
    d_pooled = dp_send[my_head * 2 // nh].astype(F32)
    for k in range(1, nh):
        d_pooled = d_pooled + dp_recv[k].astype(F32)
    arrived(dn_copies)
    mine = rows(my_head * share_h, share_h)
    d_normed = dn_send[mine, :].astype(F32)
    for k in range(1, nh):
        d_normed = d_normed + dn_recv[k].astype(F32)
    scaled = d_normed * gain
    own_unit = unit_ref[mine, :]
    back = inv_ref[mine, :][:, 0:1] * (
        scaled
        - jnp.mean(scaled, axis=-1, keepdims=True)
        - own_unit * jnp.mean(scaled * own_unit, axis=-1, keepdims=True)
    )
    left, right = d_pooled[:SLAB], d_pooled[SLAB:]
    back = back + jnp.concatenate([left, left, right, right], axis=0) * 0.25
    ig_all[mine, :] = back.astype(BF16)
    ig_copies = [
        send_head(4, k, ig_all.at[mine], ig_all.at[mine], at_head(k)) for k in range(1, nh)
    ]

    gb_shares, gb_relays = reduce_and_share(8, gb_copies, gb_part, gb_recv, gb_out, share_b)
    relay(5, ga_shares, ga_relays, ga_out, share_a)
    relay(9, gb_shares, gb_relays, gb_out, share_b)
    arrived(ig_copies)
    arrived(ga_relays)
    arrived(gb_relays)
    for copy in started:
        copy.wait_send()


def finish(
    block_ref, ig_ref, ga_ref, gb_ref, block_hbm, ig_hbm, qkv_hbm, proj_hbm, ig, qkv, proj, sems
):
    chans, wide = qkv.shape[1:]
    copies = []

    def put(src, dst):
        copy = pltpu.make_async_copy(src, dst, sems.at[len(copies)])
        copy.start()
        copies.append(copy)

    back = one_hot(token_order, TILE_H * TILE_W, transposed=True)
    ig[...] = mm(back, ig_ref[...]).astype(BF16)
    put(ig, ig_hbm)
    put(block_ref, block_hbm)
    for i in range(proj.shape[1] // wide):
        proj[:, i * wide : (i + 1) * wide] = ga_ref[
            (i + 1) * chans : (i + 2) * chans, :
        ].astype(F32)
    put(proj, proj_hbm)
    for j, part in enumerate(
        (ga_ref[0:chans, :], gb_ref[0:chans, :], gb_ref[chans : 2 * chans, :])
    ):
        qkv[j] = part.astype(F32)
        put(qkv.at[j], qkv_hbm.at[j])
    for copy in copies:
        copy.wait()


def share_of(total, n):
    return -(-total // (n * 16)) * 16


def local(n, nh, *operands):
    tokens, ln_gain, qkv, qpool, kpool, vpool, proj, skip, cot = operands
    count, wide = tokens.shape
    chans = qkv.shape[1]
    full = proj.shape[1]
    share_a = share_of(chans * (1 + full // wide), n)
    share_b = share_of(chans * 2, n)
    share_h = count // nh
    vmem = pl.BlockSpec(memory_space=pltpu.VMEM)
    hbm = pl.BlockSpec(memory_space=pltpu.HBM)
    outs = pl.pallas_call(
        functools.partial(kernel, n, nh, share_a, share_b),
        out_shape=(
            jax.ShapeDtypeStruct(cot.shape, BF16),
            jax.ShapeDtypeStruct(tokens.shape, BF16),
            jax.ShapeDtypeStruct((n * share_a, wide), BF16),
            jax.ShapeDtypeStruct((n * share_b, wide), BF16),
        ),
        in_specs=[hbm] * 9,
        out_specs=(vmem,) * 4,
        scratch_shapes=[pltpu.VMEM(x.shape, x.dtype) for x in operands]
        + [
            pltpu.VMEM((nh,) + cot.shape, BF16),
            pltpu.VMEM((2, n * SLAB, chans), BF16),
            pltpu.VMEM((2, n * SLAB, chans), BF16),
            pltpu.VMEM((2, n * SLAB, chans), BF16),
            pltpu.VMEM((2, CELLS // 2, wide), BF16),
            pltpu.VMEM((nh, CELLS // 2, wide), BF16),
            pltpu.VMEM((nh,) + cot.shape, BF16),
            pltpu.VMEM((nh,) + cot.shape, BF16),
            pltpu.VMEM((n * share_a, wide), BF16),
            pltpu.VMEM((n // 2 * share_a, wide), BF16),
            pltpu.VMEM((n // 2 * share_a, wide), BF16),
            pltpu.VMEM((n // 2, share_a, wide), BF16),
            pltpu.VMEM((n * share_b, wide), BF16),
            pltpu.VMEM((n // 2 * share_b, wide), BF16),
            pltpu.VMEM((n // 2 * share_b, wide), BF16),
            pltpu.VMEM((n // 2, share_b, wide), BF16),
            pltpu.VMEM((count, wide), BF16),
            pltpu.VMEM((nh, share_h, wide), BF16),
            pltpu.VMEM((count, wide), F32),
            pltpu.VMEM((count, 128), F32),
            pltpu.SemaphoreType.DMA((9,)),
            pltpu.SemaphoreType.DMA((10, n)),
            pltpu.SemaphoreType.DMA((10, n)),
            pltpu.SemaphoreType.DMA((5, nh)),
            pltpu.SemaphoreType.DMA((5, nh)),
        ],
        compiler_params=pltpu.CompilerParams(
            collective_id=0, has_side_effects=True, vmem_limit_bytes=40 * 1024 * 1024
        ),
    )(*[pltpu.with_memory_space_constraint(x, pltpu.HBM) for x in operands])
    return pl.pallas_call(
        finish,
        out_shape=(
            jax.ShapeDtypeStruct(cot.shape, BF16),
            jax.ShapeDtypeStruct(tokens.shape, BF16),
            jax.ShapeDtypeStruct(qkv.shape, F32),
            jax.ShapeDtypeStruct(proj.shape, F32),
        ),
        in_specs=[vmem] * 4,
        out_specs=(hbm,) * 4,
        scratch_shapes=[
            pltpu.VMEM(tokens.shape, BF16),
            pltpu.VMEM(qkv.shape, F32),
            pltpu.VMEM(proj.shape, F32),
            pltpu.SemaphoreType.DMA((6,)),
        ],
        compiler_params=pltpu.CompilerParams(vmem_limit_bytes=16 * 1024 * 1024),
    )(*outs)


def solution(mesh):
    placed = (
        P("tile", None),
        P(),
        P(None, "head", None),
        P(None, "head"),
        P(None, "head"),
        P(None, "head"),
        P("head", None),
        P("head", None),
        P("tile", "head"),
    )
    return jax.shard_map(
        functools.partial(local, mesh.shape["tile"], mesh.shape["head"]),
        mesh=mesh,
        in_specs=placed,
        out_specs=(P("tile", "head"), P("tile", None), P(None, "head", None), P("head", None)),
        check_vma=False,
    )
```

```python
import functools

import jax
import jax.numpy as jnp
from jax import lax
from jax.experimental import pallas as pl
from jax.experimental.pallas import tpu as pltpu
from jax.sharding import PartitionSpec as P

HEAD_DIM = 96
TILE_H = 8
TILE_W = 32
EPSILON = 1e-06
SLAB = TILE_H * TILE_W // 16
CELLS = SLAB * 4
MESH = pl.DeviceIdType.MESH
F32 = jnp.float32
BF16 = jnp.bfloat16


def mm(a, b, contract=(1, 0)):
    return lax.dot_general(
        a, b, (((contract[0],), (contract[1],)), ((), ())), preferred_element_type=F32
    )


def token_order(shape, dim):
    p = lax.broadcasted_iota(jnp.int32, shape, dim)
    slab, block = p >> 4, p & 15
    a, b = slab >> 2, slab & 3
    return ((block >> 3) * 4 + a) * TILE_W + (block & 7) * 4 + b


def cell_order(shape, dim):
    p = lax.broadcasted_iota(jnp.int32, shape, dim)
    slab, block = p >> 4, p & 15
    a, b = slab >> 1, slab & 1
    return ((block >> 3) * 2 + a) * (TILE_W // 2) + (block & 7) * 2 + b


def one_hot(order, size, transposed=False):
    shape = (size, size)
    dim = 1 if transposed else 0
    other = lax.broadcasted_iota(jnp.int32, shape, 1 - dim)
    return jnp.where(order(shape, dim) == other, 1.0, 0.0).astype(BF16)


def rows(start, size):
    return pl.ds(pl.multiple_of(start, 16), size)


def kernel(
    n,
    nh,
    share_a,
    share_b,
    tokens_hbm,
    gain_hbm,
    qkv_hbm,
    qpool_hbm,
    kpool_hbm,
    vpool_hbm,
    proj_hbm,
    skip_hbm,
    cot_hbm,
    block_out_ref,
    ig_all,
    ga_out,
    gb_out,
    tokens_ref,
    gain_ref,
    qkv_ref,
    qpool_ref,
    kpool_ref,
    vpool_ref,
    proj_ref,
    skip_ref,
    cot_ref,
    cot_all,
    kv_all,
    kvg_send,
    kvg_recv,
    dp_send,
    dp_recv,
    hp_send,
    hp_recv,
    ga_send,
    ga_pair,
    ga_part,
    ga_recv,
    gb_send,
    gb_pair,
    gb_part,
    gb_recv,
    dn_send,
    dn_recv,
    unit_ref,
    inv_ref,
    load_sem,
    tile_send,
    tile_recv,
    head_send,
    head_recv,
):
    me = lax.axis_index("tile")
    my_head = lax.axis_index("head")
    chips = n // 2
    chip, core = me // 2, lax.rem(me, 2)
    chans = qkv_ref.shape[1]
    wide = qkv_ref.shape[2]
    share_h = unit_ref.shape[0] // nh

    def at_tile(k):
        return (lax.rem(me + k, n), my_head)

    def at_chip(k):
        return (lax.rem(chip + k, chips) * 2 + core, my_head)

    partner = (chip * 2 + 1 - core, my_head)

    def at_head(k):
        return (me, lax.rem(my_head + k, nh))

    def send_tile(stage, k, src, dst, device):
        copy = pltpu.make_async_remote_copy(
            src_ref=src,
            dst_ref=dst,
            send_sem=tile_send.at[stage, k],
            recv_sem=tile_recv.at[stage, k],
            device_id=device,
            device_id_type=MESH,
        )
        copy.start()
        return copy

    def send_head(stage, k, src, dst, device):
        copy = pltpu.make_async_remote_copy(
            src_ref=src,
            dst_ref=dst,
            send_sem=head_send.at[stage, k],
            recv_sem=head_recv.at[stage, k],
            device_id=device,
            device_id_type=MESH,
        )
        copy.start()
        return copy

    started = []

    def arrived(copies):
        for copy in copies:
            copy.wait_recv()
        started.extend(copies)

    barrier = pltpu.get_barrier_semaphore()
    for k in range(1, n):
        pl.semaphore_signal(barrier, inc=1, device_id=at_tile(k), device_id_type=MESH)
    for k in range(1, nh):
        pl.semaphore_signal(barrier, inc=1, device_id=at_head(k), device_id_type=MESH)

    loads = {}
    for i, (name, src, dst) in enumerate(
        (
            ("cot", cot_hbm, cot_ref),
            ("tokens", tokens_hbm, tokens_ref),
            ("gain", gain_hbm, gain_ref),
            ("qkv", qkv_hbm, qkv_ref),
            ("kpool", kpool_hbm, kpool_ref),
            ("vpool", vpool_hbm, vpool_ref),
            ("qpool", qpool_hbm, qpool_ref),
            ("skip", skip_hbm, skip_ref),
            ("proj", proj_hbm, proj_ref),
        )
    ):
        loads[name] = pltpu.make_async_copy(src, dst, load_sem.at[i])
        loads[name].start()

    loads["cot"].wait()
    cot_all[my_head] = cot_ref[...]
    pl.semaphore_wait(barrier, n + nh - 2)
    cot_copies = [
        send_head(0, k, cot_ref, cot_all.at[my_head], at_head(k)) for k in range(1, nh)
    ]

    order = one_hot(token_order, TILE_H * TILE_W)
    loads["tokens"].wait()
    tokens = mm(order, tokens_ref[...])
    center = tokens - jnp.mean(tokens, axis=-1, keepdims=True)
    inv_std = lax.rsqrt(jnp.mean(center * center, axis=-1, keepdims=True) + EPSILON)
    unit = center * inv_std
    unit_ref[...] = unit
    inv_ref[...] = jnp.broadcast_to(inv_std, inv_ref.shape)
    loads["gain"].wait()
    gain = gain_ref[...].reshape(1, wide)
    normed = (unit * gain).astype(BF16)

    for name in ("qkv", "kpool", "vpool"):
        loads[name].wait()
    kpool = kpool_ref[...].astype(F32)
    vpool = vpool_ref[...].astype(F32)

    def pool_block(field, pool):
        total = pool[0:1] * field[0:SLAB]
        for s in range(1, 16):
            total = total + pool[s : s + 1] * field[s * SLAB : (s + 1) * SLAB]
        return total

    kv_all[0, 0:SLAB, :] = pool_block(mm(normed, qkv_ref[1], (1, 1)), kpool).astype(BF16)
    kv_all[1, 0:SLAB, :] = pool_block(mm(normed, qkv_ref[2], (1, 1)), vpool).astype(BF16)

    kv_copies = [
        send_tile(
            0,
            k,
            kv_all.at[:, 0:SLAB],
            kv_all.at[:, k * SLAB : (k + 1) * SLAB],
            at_tile(k),
        )
        for k in range(1, n)
    ]

    def cell_slabs(a, b):
        return [
            (2 * a2 + b2, (2 * a + a2) * 4 + 2 * b + b2) for a2 in range(2) for b2 in range(2)
        ]

    loads["qpool"].wait()
    qpool = qpool_ref[...].astype(F32)
    field = mm(normed, qkv_ref[0], (1, 1))
    query_parts = []
    input_parts = []
    for a in range(2):
        for b in range(2):
            total = None
            whole = None
            for w, s in cell_slabs(a, b):
                term = qpool[w : w + 1] * field[s * SLAB : (s + 1) * SLAB]
                total = term if total is None else total + term
                piece = tokens[s * SLAB : (s + 1) * SLAB]
                whole = piece if whole is None else whole + piece
            query_parts.append(total)
            input_parts.append(whole)
    queries_wide = jnp.concatenate(query_parts, axis=0).astype(BF16).astype(F32)
    pooled_input = (jnp.concatenate(input_parts, axis=0) * 0.25).astype(BF16)

    cells = one_hot(cell_order, CELLS)
    cells_back = one_hot(cell_order, CELLS, transposed=True)
    loads["skip"].wait()

    own_cot = mm(cells, cot_ref[...]).astype(BF16)
    d_pooled = mm(own_cot, skip_ref[...]).astype(BF16)
    half = CELLS // 2
    dp_send[0] = d_pooled[:half]
    dp_send[1] = d_pooled[half:]
    dp_copies = [
        send_head(
            1,
            k,
            dp_send.at[lax.rem(my_head + k, nh) * 2 // nh],
            dp_recv.at[k],
            at_head(k),
        )
        for k in range(1, nh)
    ]

    loads["proj"].wait()
    arrived(cot_copies)
    full_cot = jnp.concatenate([cot_all[h] for h in range(nh)], axis=1)
    full_cot = mm(cells, full_cot).astype(BF16)
    d_attended = mm(full_cot, proj_ref[...], (1, 1)).astype(BF16).astype(F32)

    heads = chans // HEAD_DIM
    lane = lax.broadcasted_iota(jnp.int32, (CELLS, chans), 1)
    masks = [
        jnp.logical_and(lane >= h * HEAD_DIM, lane < (h + 1) * HEAD_DIM) for h in range(heads)
    ]

    def by_head(x):
        return jnp.concatenate([jnp.where(m, x, 0.0) for m in masks], axis=0).astype(BF16)

    def from_heads(x):
        total = jnp.where(masks[0], x[:CELLS], 0.0)
        for h in range(1, heads):
            total = jnp.where(masks[h], x[h * CELLS : (h + 1) * CELLS], total)
        return total

    q_rows = by_head(queries_wide)
    g_rows = by_head(d_attended)

    arrived(kv_copies)
    keys = kv_all[0]
    values = kv_all[1]
    scale = HEAD_DIM ** (-0.5)
    exp_scores = jnp.exp(mm(q_rows, keys, (1, 1)) * scale)
    row_total = jnp.sum(exp_scores, axis=-1, keepdims=True)
    probs = (exp_scores / row_total).astype(BF16)
    dprobs = mm(g_rows, values, (1, 1))
    probs_wide = probs.astype(F32)
    row_delta = jnp.sum(probs_wide * dprobs, axis=-1, keepdims=True)
    d_scores = (scale * probs_wide * (dprobs - row_delta)).astype(BF16)
    key_grad = mm(d_scores, q_rows, (0, 0))
    value_grad = mm(probs, g_rows, (0, 0))
    kvg_send[0] = key_grad.astype(BF16)
    kvg_send[1] = value_grad.astype(BF16)
    kvg_copies = [
        send_tile(
            1,
            k,
            kvg_send.at[:, k * SLAB : (k + 1) * SLAB],
            kvg_recv.at[:, k * SLAB : (k + 1) * SLAB],
            at_tile(n - k),
        )
        for k in range(1, n)
    ]

    attended = (from_heads(mm(probs, values)) + queries_wide).astype(BF16)
    head_part = mm(mm(cells_back, attended).astype(BF16), proj_ref[...])
    for h in range(nh):
        hp_send[h] = head_part[:, h * chans : (h + 1) * chans].astype(BF16)
    hp_copies = [
        send_head(2, k, hp_send.at[lax.rem(my_head + k, nh)], hp_recv.at[k], at_head(k))
        for k in range(1, nh)
    ]

    query_grad = from_heads(mm(d_scores, keys)) + d_attended
    spread = []
    for s in range(16):
        a, b = s // 4, s % 4
        cell = (a // 2) * 2 + b // 2
        w = (a % 2) * 2 + b % 2
        spread.append(qpool[w : w + 1] * query_grad[cell * SLAB : (cell + 1) * SLAB])
    d_projected = jnp.concatenate(spread, axis=0).astype(BF16)
    ga_send[0:chans, :] = mm(d_projected, normed, (0, 0)).astype(BF16)
    proj_part = mm(attended, full_cot, (0, 0)).astype(BF16)
    halves = proj_part.shape[1] // wide
    for i in range(halves):
        ga_send[(i + 1) * chans : (i + 2) * chans, :] = proj_part[:, i * wide : (i + 1) * wide]
    filled = (halves + 1) * chans
    if ga_send.shape[0] > filled:
        ga_send[filled:, :] = jnp.zeros((ga_send.shape[0] - filled, wide), BF16)
    half_a, half_b = chips * share_a, chips * share_b
    ga_pairs = [
        send_tile(2, 1, ga_send.at[rows((1 - core) * half_a, half_a)], ga_pair, partner)
    ]
    d_normed = mm(d_projected, qkv_ref[0])

    def fold(stage, pairs, sent, pair, part, received, share):
        arrived(pairs)
        size = chips * share
        total = sent[rows(core * size, size), :].astype(F32) + pair[...].astype(F32)
        part[...] = total.astype(BF16)
        return [
            send_tile(
                stage,
                k,
                part.at[rows(lax.rem(chip + k, chips) * share, share)],
                received.at[k],
                at_chip(k),
            )
            for k in range(1, chips)
        ]

    def place(k, share):
        from_chip = lax.rem(chip + chips - k, chips)
        return rows((core * chips + from_chip) * share, share)

    def reduce_and_share(stage, copies, part, received, out, share):
        arrived(copies)
        total = part[rows(chip * share, share), :].astype(F32)
        for k in range(1, chips):
            total = total + received[k].astype(F32)
        mine = place(0, share)
        out[mine, :] = total.astype(BF16)
        shares = [
            send_tile(stage, k, out.at[mine], out.at[mine], at_chip(k))
            for k in range(1, chips)
        ]
        relays = [send_tile(stage + 1, 0, out.at[mine], out.at[mine], partner)]
        return shares, relays

    def relay(stage, shares, relays, out, share):
        for k in range(1, chips):
            arrived(shares[k - 1 : k])
            there = place(k, share)
            relays.append(send_tile(stage, k, out.at[there], out.at[there], partner))

    ga_copies = fold(3, ga_pairs, ga_send, ga_pair, ga_part, ga_recv, share_a)

    arrived(kvg_copies)
    d_fields = []
    for j, pool, own in ((0, kpool, key_grad), (1, vpool, value_grad)):
        total = own[0:SLAB]
        for k in range(1, n):
            total = total + kvg_recv[j, k * SLAB : (k + 1) * SLAB, :].astype(F32)
        d_projected = jnp.concatenate([pool[s : s + 1] * total for s in range(16)], axis=0)
        d_fields.append(d_projected.astype(BF16))
        d_normed = d_normed + mm(d_fields[j], qkv_ref[j + 1])
    dn_send[...] = d_normed.astype(BF16)
    piece = share_h // 2
    dn_copies = [
        [
            send_head(
                3 + half,
                k,
                dn_send.at[rows(lax.rem(my_head + k, nh) * share_h + half * piece, piece)],
                dn_recv.at[k, half * piece : (half + 1) * piece],
                at_head(k),
            )
            for k in range(1, nh)
        ]
        for half in range(2)
    ]
    for j in range(2):
        gb_send[j * chans : (j + 1) * chans, :] = mm(d_fields[j], normed, (0, 0)).astype(BF16)
    filled = 2 * chans
    if gb_send.shape[0] > filled:
        gb_send[filled:, :] = jnp.zeros((gb_send.shape[0] - filled, wide), BF16)
    gb_pairs = [
        send_tile(6, 1, gb_send.at[rows((1 - core) * half_b, half_b)], gb_pair, partner)
    ]

    gb_copies = fold(7, gb_pairs, gb_send, gb_pair, gb_part, gb_recv, share_b)
    ga_shares, ga_relays = reduce_and_share(4, ga_copies, ga_part, ga_recv, ga_out, share_a)

    pooled_input = mm(cells_back, pooled_input).astype(BF16)
    skipped = mm(pooled_input, skip_ref[...], (1, 1))
    arrived(hp_copies)
    summed = hp_send[my_head].astype(F32)
    for k in range(1, nh):
        summed = summed + hp_recv[k].astype(F32)
    block_out_ref[...] = (summed + skipped).astype(BF16)

    arrived(dp_copies)
    d_pooled = dp_send[my_head * 2 // nh].astype(F32)
    for k in range(1, nh):
        d_pooled = d_pooled + dp_recv[k].astype(F32)
    d_pooled = d_pooled * 0.25

    def share_input(half):
        arrived(dn_copies[half])
        mine = rows(my_head * share_h + half * piece, piece)
        d_normed = dn_send[mine, :].astype(F32)
        for k in range(1, nh):
            d_normed = d_normed + dn_recv[k, half * piece : (half + 1) * piece, :].astype(F32)
        scaled = d_normed * gain
        own_unit = unit_ref[mine, :]
        back = inv_ref[mine, :][:, 0:1] * (
            scaled
            - jnp.mean(scaled, axis=-1, keepdims=True)
            - own_unit * jnp.mean(scaled * own_unit, axis=-1, keepdims=True)
        )
        cell = d_pooled[half * SLAB : (half + 1) * SLAB]
        ig_all[mine, :] = (back + jnp.concatenate([cell, cell], axis=0)).astype(BF16)
        return [
            send_head(5 + half, k, ig_all.at[mine], ig_all.at[mine], at_head(k))
            for k in range(1, nh)
        ]

    ig_copies = share_input(0)
    gb_shares, gb_relays = reduce_and_share(8, gb_copies, gb_part, gb_recv, gb_out, share_b)
    ig_copies += share_input(1)
    relay(5, ga_shares, ga_relays, ga_out, share_a)
    relay(9, gb_shares, gb_relays, gb_out, share_b)
    arrived(ig_copies)
    arrived(ga_relays)
    arrived(gb_relays)
    for copy in started:
        copy.wait_send()


def finish(
    block_ref, ig_ref, ga_ref, gb_ref, block_hbm, ig_hbm, qkv_hbm, proj_hbm, ig, qkv, proj, sems
):
    chans, wide = qkv.shape[1:]
    copies = []

    def put(src, dst):
        copy = pltpu.make_async_copy(src, dst, sems.at[len(copies)])
        copy.start()
        copies.append(copy)

    back = one_hot(token_order, TILE_H * TILE_W, transposed=True)
    ig[...] = mm(back, ig_ref[...]).astype(BF16)
    put(ig, ig_hbm)
    put(block_ref, block_hbm)
    for i in range(proj.shape[1] // wide):
        proj[:, i * wide : (i + 1) * wide] = ga_ref[
            (i + 1) * chans : (i + 2) * chans, :
        ].astype(F32)
    put(proj, proj_hbm)
    for j, part in enumerate(
        (ga_ref[0:chans, :], gb_ref[0:chans, :], gb_ref[chans : 2 * chans, :])
    ):
        qkv[j] = part.astype(F32)
        put(qkv.at[j], qkv_hbm.at[j])
    for copy in copies:
        copy.wait()


def share_of(total, n):
    return -(-total // (n * 16)) * 16


def local(n, nh, *operands):
    tokens, ln_gain, qkv, qpool, kpool, vpool, proj, skip, cot = operands
    count, wide = tokens.shape
    chans = qkv.shape[1]
    full = proj.shape[1]
    share_a = share_of(chans * (1 + full // wide), n)
    share_b = share_of(chans * 2, n)
    share_h = count // nh
    vmem = pl.BlockSpec(memory_space=pltpu.VMEM)
    hbm = pl.BlockSpec(memory_space=pltpu.HBM)
    outs = pl.pallas_call(
        functools.partial(kernel, n, nh, share_a, share_b),
        out_shape=(
            jax.ShapeDtypeStruct(cot.shape, BF16),
            jax.ShapeDtypeStruct(tokens.shape, BF16),
            jax.ShapeDtypeStruct((n * share_a, wide), BF16),
            jax.ShapeDtypeStruct((n * share_b, wide), BF16),
        ),
        in_specs=[hbm] * 9,
        out_specs=(vmem,) * 4,
        scratch_shapes=[pltpu.VMEM(x.shape, x.dtype) for x in operands]
        + [
            pltpu.VMEM((nh,) + cot.shape, BF16),
            pltpu.VMEM((2, n * SLAB, chans), BF16),
            pltpu.VMEM((2, n * SLAB, chans), BF16),
            pltpu.VMEM((2, n * SLAB, chans), BF16),
            pltpu.VMEM((2, CELLS // 2, wide), BF16),
            pltpu.VMEM((nh, CELLS // 2, wide), BF16),
            pltpu.VMEM((nh,) + cot.shape, BF16),
            pltpu.VMEM((nh,) + cot.shape, BF16),
            pltpu.VMEM((n * share_a, wide), BF16),
            pltpu.VMEM((n // 2 * share_a, wide), BF16),
            pltpu.VMEM((n // 2 * share_a, wide), BF16),
            pltpu.VMEM((n // 2, share_a, wide), BF16),
            pltpu.VMEM((n * share_b, wide), BF16),
            pltpu.VMEM((n // 2 * share_b, wide), BF16),
            pltpu.VMEM((n // 2 * share_b, wide), BF16),
            pltpu.VMEM((n // 2, share_b, wide), BF16),
            pltpu.VMEM((count, wide), BF16),
            pltpu.VMEM((nh, share_h, wide), BF16),
            pltpu.VMEM((count, wide), F32),
            pltpu.VMEM((count, 128), F32),
            pltpu.SemaphoreType.DMA((9,)),
            pltpu.SemaphoreType.DMA((10, n)),
            pltpu.SemaphoreType.DMA((10, n)),
            pltpu.SemaphoreType.DMA((7, nh)),
            pltpu.SemaphoreType.DMA((7, nh)),
        ],
        compiler_params=pltpu.CompilerParams(
            collective_id=0, has_side_effects=True, vmem_limit_bytes=40 * 1024 * 1024
        ),
    )(*[pltpu.with_memory_space_constraint(x, pltpu.HBM) for x in operands])
    return pl.pallas_call(
        finish,
        out_shape=(
            jax.ShapeDtypeStruct(cot.shape, BF16),
            jax.ShapeDtypeStruct(tokens.shape, BF16),
            jax.ShapeDtypeStruct(qkv.shape, F32),
            jax.ShapeDtypeStruct(proj.shape, F32),
        ),
        in_specs=[vmem] * 4,
        out_specs=(hbm,) * 4,
        scratch_shapes=[
            pltpu.VMEM(tokens.shape, BF16),
            pltpu.VMEM(qkv.shape, F32),
            pltpu.VMEM(proj.shape, F32),
            pltpu.SemaphoreType.DMA((6,)),
        ],
        compiler_params=pltpu.CompilerParams(vmem_limit_bytes=16 * 1024 * 1024),
    )(*outs)


def solution(mesh):
    placed = (
        P("tile", None),
        P(),
        P(None, "head", None),
        P(None, "head"),
        P(None, "head"),
        P(None, "head"),
        P("head", None),
        P("head", None),
        P("tile", "head"),
    )
    return jax.shard_map(
        functools.partial(local, mesh.shape["tile"], mesh.shape["head"]),
        mesh=mesh,
        in_specs=placed,
        out_specs=(P("tile", "head"), P("tile", None), P(None, "head", None), P("head", None)),
        check_vma=False,
    )
```

```python
import functools

import jax
import jax.numpy as jnp
from jax import lax
from jax.experimental import pallas as pl
from jax.experimental.pallas import tpu as pltpu
from jax.sharding import PartitionSpec as P

HEAD_DIM = 96
TILE_H = 8
TILE_W = 32
EPSILON = 1e-06
SLAB = TILE_H * TILE_W // 16
CELLS = SLAB * 4
MESH = pl.DeviceIdType.MESH
F32 = jnp.float32
BF16 = jnp.bfloat16


def mm(a, b, contract=(1, 0)):
    return lax.dot_general(
        a, b, (((contract[0],), (contract[1],)), ((), ())), preferred_element_type=F32
    )


def token_order(shape, dim):
    p = lax.broadcasted_iota(jnp.int32, shape, dim)
    slab, block = p >> 4, p & 15
    a, b = slab >> 2, slab & 3
    return ((block >> 3) * 4 + a) * TILE_W + (block & 7) * 4 + b


def cell_order(shape, dim):
    p = lax.broadcasted_iota(jnp.int32, shape, dim)
    slab, block = p >> 4, p & 15
    a, b = slab >> 1, slab & 1
    return ((block >> 3) * 2 + a) * (TILE_W // 2) + (block & 7) * 2 + b


def one_hot(order, size, transposed=False):
    shape = (size, size)
    dim = 1 if transposed else 0
    other = lax.broadcasted_iota(jnp.int32, shape, 1 - dim)
    return jnp.where(order(shape, dim) == other, 1.0, 0.0).astype(BF16)


def rows(start, size):
    return pl.ds(pl.multiple_of(start, 16), size)


def kernel(
    n,
    nh,
    share_a,
    share_b,
    tokens_hbm,
    gain_hbm,
    qkv_hbm,
    qpool_hbm,
    kpool_hbm,
    vpool_hbm,
    proj_hbm,
    skip_hbm,
    cot_hbm,
    block_out_ref,
    ig_all,
    ga_out,
    gb_out,
    tokens_ref,
    gain_ref,
    qkv_ref,
    qpool_ref,
    kpool_ref,
    vpool_ref,
    proj_ref,
    skip_ref,
    cot_ref,
    cot_all,
    kv_all,
    kvg_send,
    kvg_recv,
    dp_send,
    dp_recv,
    hp_send,
    hp_recv,
    ga_send,
    ga_pair,
    ga_part,
    ga_recv,
    gb_send,
    gb_pair,
    gb_part,
    gb_recv,
    dn_send,
    dn_recv,
    unit_ref,
    inv_ref,
    load_sem,
    tile_send,
    tile_recv,
    head_send,
    head_recv,
):
    me = lax.axis_index("tile")
    my_head = lax.axis_index("head")
    chips = n // 2
    chip, core = me // 2, lax.rem(me, 2)
    chans = qkv_ref.shape[1]
    wide = qkv_ref.shape[2]
    share_h = unit_ref.shape[0] // nh

    def at_tile(k):
        return (lax.rem(me + k, n), my_head)

    def at_chip(k):
        return (lax.rem(chip + k, chips) * 2 + core, my_head)

    partner = (chip * 2 + 1 - core, my_head)

    groups = nh // 2
    group, bit = my_head // 2, lax.rem(my_head, 2)
    side = (me, group * 2 + 1 - bit)

    def at_group(k):
        return (me, lax.rem(group + k, groups) * 2 + bit)

    def at_head(k):
        return (me, lax.rem(my_head + k, nh))

    def send_tile(stage, k, src, dst, device):
        copy = pltpu.make_async_remote_copy(
            src_ref=src,
            dst_ref=dst,
            send_sem=tile_send.at[stage, k],
            recv_sem=tile_recv.at[stage, k],
            device_id=device,
            device_id_type=MESH,
        )
        copy.start()
        return copy

    def send_head(stage, k, src, dst, device):
        copy = pltpu.make_async_remote_copy(
            src_ref=src,
            dst_ref=dst,
            send_sem=head_send.at[stage, k],
            recv_sem=head_recv.at[stage, k],
            device_id=device,
            device_id_type=MESH,
        )
        copy.start()
        return copy

    started = []

    def arrived(copies):
        for copy in copies:
            copy.wait_recv()
        started.extend(copies)

    barrier = pltpu.get_barrier_semaphore()
    for k in range(1, n):
        pl.semaphore_signal(barrier, inc=1, device_id=at_tile(k), device_id_type=MESH)
    for k in range(1, nh):
        pl.semaphore_signal(barrier, inc=1, device_id=at_head(k), device_id_type=MESH)

    loads = {}
    for i, (name, src, dst) in enumerate(
        (
            ("cot", cot_hbm, cot_ref),
            ("tokens", tokens_hbm, tokens_ref),
            ("gain", gain_hbm, gain_ref),
            ("qkv", qkv_hbm, qkv_ref),
            ("kpool", kpool_hbm, kpool_ref),
            ("vpool", vpool_hbm, vpool_ref),
            ("qpool", qpool_hbm, qpool_ref),
            ("skip", skip_hbm, skip_ref),
            ("proj", proj_hbm, proj_ref),
        )
    ):
        loads[name] = pltpu.make_async_copy(src, dst, load_sem.at[i])
        loads[name].start()

    order = one_hot(token_order, TILE_H * TILE_W)
    loads["cot"].wait()
    cot_all[my_head] = cot_ref[...]
    pl.semaphore_wait(barrier, n + nh - 2)
    cot_copies = [
        send_head(0, k, cot_ref, cot_all.at[my_head], at_head(k)) for k in range(1, nh)
    ]

    loads["tokens"].wait()
    tokens = mm(order, tokens_ref[...])
    center = tokens - jnp.mean(tokens, axis=-1, keepdims=True)
    inv_std = lax.rsqrt(jnp.mean(center * center, axis=-1, keepdims=True) + EPSILON)
    unit = center * inv_std
    unit_ref[...] = unit
    inv_ref[...] = jnp.broadcast_to(inv_std, inv_ref.shape)
    loads["gain"].wait()
    gain = gain_ref[...].reshape(1, wide)
    normed = (unit * gain).astype(BF16)

    for name in ("qkv", "kpool", "vpool"):
        loads[name].wait()
    kpool = kpool_ref[...].astype(F32)
    vpool = vpool_ref[...].astype(F32)

    def pool_block(field, pool):
        total = pool[0:1] * field[0:SLAB]
        for s in range(1, 16):
            total = total + pool[s : s + 1] * field[s * SLAB : (s + 1) * SLAB]
        return total

    kv_all[0, 0:SLAB, :] = pool_block(mm(normed, qkv_ref[1], (1, 1)), kpool).astype(BF16)
    kv_all[1, 0:SLAB, :] = pool_block(mm(normed, qkv_ref[2], (1, 1)), vpool).astype(BF16)

    kv_copies = [
        send_tile(
            0,
            k,
            kv_all.at[:, 0:SLAB],
            kv_all.at[:, k * SLAB : (k + 1) * SLAB],
            at_tile(k),
        )
        for k in range(1, n)
    ]

    def cell_slabs(a, b):
        return [
            (2 * a2 + b2, (2 * a + a2) * 4 + 2 * b + b2) for a2 in range(2) for b2 in range(2)
        ]

    loads["qpool"].wait()
    qpool = qpool_ref[...].astype(F32)
    field = mm(normed, qkv_ref[0], (1, 1))
    query_parts = []
    input_parts = []
    for a in range(2):
        for b in range(2):
            total = None
            whole = None
            for w, s in cell_slabs(a, b):
                term = qpool[w : w + 1] * field[s * SLAB : (s + 1) * SLAB]
                total = term if total is None else total + term
                piece = tokens[s * SLAB : (s + 1) * SLAB]
                whole = piece if whole is None else whole + piece
            query_parts.append(total)
            input_parts.append(whole)
    queries_wide = jnp.concatenate(query_parts, axis=0).astype(BF16).astype(F32)
    pooled_input = (jnp.concatenate(input_parts, axis=0) * 0.25).astype(BF16)

    cells = one_hot(cell_order, CELLS)
    cells_back = one_hot(cell_order, CELLS, transposed=True)
    loads["skip"].wait()

    own_cot = mm(cells, cot_ref[...]).astype(BF16)
    d_pooled = mm(own_cot, skip_ref[...]).astype(BF16)
    half = CELLS // 2
    dp_send[0] = d_pooled[:half]
    dp_send[1] = d_pooled[half:]
    dp_copies = [
        send_head(
            1,
            k,
            dp_send.at[lax.rem(my_head + k, nh) * 2 // nh],
            dp_recv.at[k],
            at_head(k),
        )
        for k in range(1, nh)
    ]

    loads["proj"].wait()
    arrived(cot_copies)
    full_cot = jnp.concatenate([cot_all[h] for h in range(nh)], axis=1)
    full_cot = mm(cells, full_cot).astype(BF16)
    d_attended = mm(full_cot, proj_ref[...], (1, 1)).astype(BF16).astype(F32)

    heads = chans // HEAD_DIM
    lane = lax.broadcasted_iota(jnp.int32, (CELLS, chans), 1)
    masks = [
        jnp.logical_and(lane >= h * HEAD_DIM, lane < (h + 1) * HEAD_DIM) for h in range(heads)
    ]

    def by_head(x):
        return jnp.concatenate([jnp.where(m, x, 0.0) for m in masks], axis=0).astype(BF16)

    def from_heads(x):
        total = jnp.where(masks[0], x[:CELLS], 0.0)
        for h in range(1, heads):
            total = jnp.where(masks[h], x[h * CELLS : (h + 1) * CELLS], total)
        return total

    q_rows = by_head(queries_wide)
    g_rows = by_head(d_attended)

    arrived(kv_copies)
    keys = kv_all[0]
    values = kv_all[1]
    scale = HEAD_DIM ** (-0.5)
    exp_scores = jnp.exp(mm(keys, q_rows, (1, 1)) * scale)
    row_total = jnp.sum(exp_scores, axis=0, keepdims=True)
    probs = (exp_scores / row_total).astype(BF16)
    dprobs = mm(values, g_rows, (1, 1))
    probs_wide = probs.astype(F32)
    row_delta = jnp.sum(probs_wide * dprobs, axis=0, keepdims=True)
    d_scores = (scale * probs_wide * (dprobs - row_delta)).astype(BF16)
    key_grad = mm(d_scores, q_rows)
    value_grad = mm(probs, g_rows)
    kvg_send[0] = key_grad.astype(BF16)
    kvg_send[1] = value_grad.astype(BF16)
    kvg_copies = [
        send_tile(
            1,
            k,
            kvg_send.at[:, k * SLAB : (k + 1) * SLAB],
            kvg_recv.at[:, k * SLAB : (k + 1) * SLAB],
            at_tile(n - k),
        )
        for k in range(1, n)
    ]

    attended = (from_heads(mm(probs, values, (0, 0))) + queries_wide).astype(BF16)
    head_part = mm(mm(cells_back, attended).astype(BF16), proj_ref[...])
    for h in range(nh):
        hp_send[h] = head_part[:, h * chans : (h + 1) * chans].astype(BF16)
    hp_copies = [
        send_head(2, k, hp_send.at[lax.rem(my_head + k, nh)], hp_recv.at[k], at_head(k))
        for k in range(1, nh)
    ]

    query_grad = from_heads(mm(d_scores, keys, (0, 0))) + d_attended
    spread = []
    for s in range(16):
        a, b = s // 4, s % 4
        cell = (a // 2) * 2 + b // 2
        w = (a % 2) * 2 + b % 2
        spread.append(qpool[w : w + 1] * query_grad[cell * SLAB : (cell + 1) * SLAB])
    d_projected = jnp.concatenate(spread, axis=0).astype(BF16)
    ga_send[0:chans, :] = mm(d_projected, normed, (0, 0)).astype(BF16)
    proj_part = mm(attended, full_cot, (0, 0)).astype(BF16)
    halves = proj_part.shape[1] // wide
    for i in range(halves):
        ga_send[(i + 1) * chans : (i + 2) * chans, :] = proj_part[:, i * wide : (i + 1) * wide]
    filled = (halves + 1) * chans
    if ga_send.shape[0] > filled:
        ga_send[filled:, :] = jnp.zeros((ga_send.shape[0] - filled, wide), BF16)
    half_a, half_b = chips * share_a, chips * share_b
    ga_pairs = [
        send_tile(2, 1, ga_send.at[rows((1 - core) * half_a, half_a)], ga_pair, partner)
    ]
    d_normed = mm(d_projected, qkv_ref[0])

    def fold(stage, pairs, sent, pair, part, received, share):
        arrived(pairs)
        size = chips * share
        total = sent[rows(core * size, size), :].astype(F32) + pair[...].astype(F32)
        part[...] = total.astype(BF16)
        return [
            send_tile(
                stage,
                k,
                part.at[rows(lax.rem(chip + k, chips) * share, share)],
                received.at[k],
                at_chip(k),
            )
            for k in range(1, chips)
        ]

    def place(k, share):
        from_chip = lax.rem(chip + chips - k, chips)
        return rows((core * chips + from_chip) * share, share)

    def reduce_and_share(stage, copies, part, received, out, share):
        arrived(copies)
        total = part[rows(chip * share, share), :].astype(F32)
        for k in range(1, chips):
            total = total + received[k].astype(F32)
        mine = place(0, share)
        out[mine, :] = total.astype(BF16)
        shares = [
            send_tile(stage, k, out.at[mine], out.at[mine], at_chip(k))
            for k in range(1, chips)
        ]
        relays = [send_tile(stage + 1, 0, out.at[mine], out.at[mine], partner)]
        return shares, relays

    def relay(stage, shares, relays, out, share):
        for k in range(1, chips):
            arrived(shares[k - 1 : k])
            there = place(k, share)
            relays.append(send_tile(stage, k, out.at[there], out.at[there], partner))

    ga_copies = fold(3, ga_pairs, ga_send, ga_pair, ga_part, ga_recv, share_a)

    arrived(kvg_copies)
    d_fields = []
    for j, pool, own in ((0, kpool, key_grad), (1, vpool, value_grad)):
        total = own[0:SLAB]
        for k in range(1, n):
            total = total + kvg_recv[j, k * SLAB : (k + 1) * SLAB, :].astype(F32)
        d_projected = jnp.concatenate([pool[s : s + 1] * total for s in range(16)], axis=0)
        d_fields.append(d_projected.astype(BF16))
        d_normed = d_normed + mm(d_fields[j], qkv_ref[j + 1])
    dn_send[...] = d_normed.astype(BF16)
    piece = share_h // 2
    dn_copies = [
        [
            send_head(
                3 + half,
                k,
                dn_send.at[rows(lax.rem(my_head + k, nh) * share_h + half * piece, piece)],
                dn_recv.at[k, half * piece : (half + 1) * piece],
                at_head(k),
            )
            for k in range(1, nh)
        ]
        for half in range(2)
    ]
    for j in range(2):
        gb_send[j * chans : (j + 1) * chans, :] = mm(d_fields[j], normed, (0, 0)).astype(BF16)
    filled = 2 * chans
    if gb_send.shape[0] > filled:
        gb_send[filled:, :] = jnp.zeros((gb_send.shape[0] - filled, wide), BF16)
    gb_pairs = [
        send_tile(6, 1, gb_send.at[rows((1 - core) * half_b, half_b)], gb_pair, partner)
    ]

    pooled_input = mm(cells_back, pooled_input).astype(BF16)
    skipped = mm(pooled_input, skip_ref[...], (1, 1))
    arrived(dp_copies)
    d_pooled = dp_send[my_head * 2 // nh].astype(F32)
    for k in range(1, nh):
        d_pooled = d_pooled + dp_recv[k].astype(F32)
    d_pooled = d_pooled * 0.25

    gb_copies = fold(7, gb_pairs, gb_send, gb_pair, gb_part, gb_recv, share_b)
    ga_shares, ga_relays = reduce_and_share(4, ga_copies, ga_part, ga_recv, ga_out, share_a)

    arrived(hp_copies)
    summed = hp_send[my_head].astype(F32)
    for k in range(1, nh):
        summed = summed + hp_recv[k].astype(F32)
    block_out_ref[...] = (summed + skipped).astype(BF16)

    def share_input(half):
        arrived(dn_copies[half])
        mine = rows(my_head * share_h + half * piece, piece)
        d_normed = dn_send[mine, :].astype(F32)
        for k in range(1, nh):
            d_normed = d_normed + dn_recv[k, half * piece : (half + 1) * piece, :].astype(F32)
        scaled = d_normed * gain
        own_unit = unit_ref[mine, :]
        back = inv_ref[mine, :][:, 0:1] * (
            scaled
            - jnp.mean(scaled, axis=-1, keepdims=True)
            - own_unit * jnp.mean(scaled * own_unit, axis=-1, keepdims=True)
        )
        cell = d_pooled[half * SLAB : (half + 1) * SLAB]
        ig_all[mine, :] = (back + jnp.concatenate([cell, cell], axis=0)).astype(BF16)
        far = [
            send_head(5 + half, k, ig_all.at[mine], ig_all.at[mine], at_group(k))
            for k in range(1, groups)
        ]
        return far, [send_head(7 + half, 0, ig_all.at[mine], ig_all.at[mine], side)]

    def relay_input(half, far, near):
        for k in range(1, groups):
            arrived(far[k - 1 : k])
            owner = lax.rem(group + groups - k, groups) * 2 + bit
            there = rows(owner * share_h + half * piece, piece)
            near.append(send_head(7 + half, k, ig_all.at[there], ig_all.at[there], side))

    first_far, first_near = share_input(0)
    gb_shares, gb_relays = reduce_and_share(8, gb_copies, gb_part, gb_recv, gb_out, share_b)
    last_far, last_near = share_input(1)
    relay(5, ga_shares, ga_relays, ga_out, share_a)
    relay_input(0, first_far, first_near)
    relay(9, gb_shares, gb_relays, gb_out, share_b)
    relay_input(1, last_far, last_near)
    arrived(first_near)
    arrived(last_near)
    arrived(ga_relays)
    arrived(gb_relays)
    for copy in started:
        copy.wait_send()


def finish(
    block_ref, ig_ref, ga_ref, gb_ref, block_hbm, ig_hbm, qkv_hbm, proj_hbm, ig, qkv, proj, sems
):
    chans, wide = qkv.shape[1:]
    copies = []

    def put(src, dst):
        copy = pltpu.make_async_copy(src, dst, sems.at[len(copies)])
        copy.start()
        copies.append(copy)

    back = one_hot(token_order, TILE_H * TILE_W, transposed=True)
    ig[...] = mm(back, ig_ref[...]).astype(BF16)
    put(ig, ig_hbm)
    put(block_ref, block_hbm)
    for i in range(proj.shape[1] // wide):
        proj[:, i * wide : (i + 1) * wide] = ga_ref[
            (i + 1) * chans : (i + 2) * chans, :
        ].astype(F32)
    put(proj, proj_hbm)
    for j, part in enumerate(
        (ga_ref[0:chans, :], gb_ref[0:chans, :], gb_ref[chans : 2 * chans, :])
    ):
        qkv[j] = part.astype(F32)
        put(qkv.at[j], qkv_hbm.at[j])
    for copy in copies:
        copy.wait()


def share_of(total, n):
    return -(-total // (n * 16)) * 16


def local(n, nh, *operands):
    tokens, ln_gain, qkv, qpool, kpool, vpool, proj, skip, cot = operands
    count, wide = tokens.shape
    chans = qkv.shape[1]
    full = proj.shape[1]
    share_a = share_of(chans * (1 + full // wide), n)
    share_b = share_of(chans * 2, n)
    share_h = count // nh
    vmem = pl.BlockSpec(memory_space=pltpu.VMEM)
    hbm = pl.BlockSpec(memory_space=pltpu.HBM)
    outs = pl.pallas_call(
        functools.partial(kernel, n, nh, share_a, share_b),
        out_shape=(
            jax.ShapeDtypeStruct(cot.shape, BF16),
            jax.ShapeDtypeStruct(tokens.shape, BF16),
            jax.ShapeDtypeStruct((n * share_a, wide), BF16),
            jax.ShapeDtypeStruct((n * share_b, wide), BF16),
        ),
        in_specs=[hbm] * 9,
        out_specs=(vmem,) * 4,
        scratch_shapes=[pltpu.VMEM(x.shape, x.dtype) for x in operands]
        + [
            pltpu.VMEM((nh,) + cot.shape, BF16),
            pltpu.VMEM((2, n * SLAB, chans), BF16),
            pltpu.VMEM((2, n * SLAB, chans), BF16),
            pltpu.VMEM((2, n * SLAB, chans), BF16),
            pltpu.VMEM((2, CELLS // 2, wide), BF16),
            pltpu.VMEM((nh, CELLS // 2, wide), BF16),
            pltpu.VMEM((nh,) + cot.shape, BF16),
            pltpu.VMEM((nh,) + cot.shape, BF16),
            pltpu.VMEM((n * share_a, wide), BF16),
            pltpu.VMEM((n // 2 * share_a, wide), BF16),
            pltpu.VMEM((n // 2 * share_a, wide), BF16),
            pltpu.VMEM((n // 2, share_a, wide), BF16),
            pltpu.VMEM((n * share_b, wide), BF16),
            pltpu.VMEM((n // 2 * share_b, wide), BF16),
            pltpu.VMEM((n // 2 * share_b, wide), BF16),
            pltpu.VMEM((n // 2, share_b, wide), BF16),
            pltpu.VMEM((count, wide), BF16),
            pltpu.VMEM((nh, share_h, wide), BF16),
            pltpu.VMEM((count, wide), F32),
            pltpu.VMEM((count, 128), F32),
            pltpu.SemaphoreType.DMA((9,)),
            pltpu.SemaphoreType.DMA((10, n)),
            pltpu.SemaphoreType.DMA((10, n)),
            pltpu.SemaphoreType.DMA((9, nh)),
            pltpu.SemaphoreType.DMA((9, nh)),
        ],
        compiler_params=pltpu.CompilerParams(
            collective_id=0, has_side_effects=True, vmem_limit_bytes=40 * 1024 * 1024
        ),
    )(*[pltpu.with_memory_space_constraint(x, pltpu.HBM) for x in operands])
    return pl.pallas_call(
        finish,
        out_shape=(
            jax.ShapeDtypeStruct(cot.shape, BF16),
            jax.ShapeDtypeStruct(tokens.shape, BF16),
            jax.ShapeDtypeStruct(qkv.shape, F32),
            jax.ShapeDtypeStruct(proj.shape, F32),
        ),
        in_specs=[vmem] * 4,
        out_specs=(hbm,) * 4,
        scratch_shapes=[
            pltpu.VMEM(tokens.shape, BF16),
            pltpu.VMEM(qkv.shape, F32),
            pltpu.VMEM(proj.shape, F32),
            pltpu.SemaphoreType.DMA((6,)),
        ],
        compiler_params=pltpu.CompilerParams(vmem_limit_bytes=16 * 1024 * 1024),
    )(*outs)


def solution(mesh):
    placed = (
        P("tile", None),
        P(),
        P(None, "head", None),
        P(None, "head"),
        P(None, "head"),
        P(None, "head"),
        P("head", None),
        P("head", None),
        P("tile", "head"),
    )
    return jax.shard_map(
        functools.partial(local, mesh.shape["tile"], mesh.shape["head"]),
        mesh=mesh,
        in_specs=placed,
        out_specs=(P("tile", "head"), P("tile", None), P(None, "head", None), P("head", None)),
        check_vma=False,
    )
```

```python
import functools

import jax
import jax.numpy as jnp
from jax import lax
from jax.experimental import pallas as pl
from jax.experimental.pallas import tpu as pltpu
from jax.sharding import PartitionSpec as P

HEAD_DIM = 96
TILE_H = 8
TILE_W = 32
EPSILON = 1e-06
SLAB = TILE_H * TILE_W // 16
CELLS = SLAB * 4
MESH = pl.DeviceIdType.MESH
F32 = jnp.float32
BF16 = jnp.bfloat16


def mm(a, b, contract=(1, 0)):
    return lax.dot_general(
        a, b, (((contract[0],), (contract[1],)), ((), ())), preferred_element_type=F32
    )


def token_order(shape, dim):
    p = lax.broadcasted_iota(jnp.int32, shape, dim)
    slab, block = p >> 4, p & 15
    a, b = slab >> 2, slab & 3
    return ((block >> 3) * 4 + a) * TILE_W + (block & 7) * 4 + b


def cell_order(shape, dim):
    p = lax.broadcasted_iota(jnp.int32, shape, dim)
    slab, block = p >> 4, p & 15
    a, b = slab >> 1, slab & 1
    return ((block >> 3) * 2 + a) * (TILE_W // 2) + (block & 7) * 2 + b


def one_hot(order, size, transposed=False):
    shape = (size, size)
    dim = 1 if transposed else 0
    other = lax.broadcasted_iota(jnp.int32, shape, 1 - dim)
    return jnp.where(order(shape, dim) == other, 1.0, 0.0).astype(BF16)


def rows(start, size):
    return pl.ds(pl.multiple_of(start, 16), size)


def kernel(
    n,
    nh,
    share_a,
    share_b,
    tokens_hbm,
    gain_hbm,
    qkv_hbm,
    qpool_hbm,
    kpool_hbm,
    vpool_hbm,
    proj_hbm,
    skip_hbm,
    cot_hbm,
    block_out_ref,
    ig_all,
    ga_out,
    gb_out,
    tokens_ref,
    gain_ref,
    qkv_ref,
    qpool_ref,
    kpool_ref,
    vpool_ref,
    proj_ref,
    skip_ref,
    cot_ref,
    cot_all,
    kv_all,
    kvg_send,
    kvg_recv,
    dp_send,
    dp_recv,
    hp_send,
    hp_recv,
    ga_send,
    ga_pair,
    ga_part,
    ga_recv,
    gb_send,
    gb_recv,
    dn_send,
    dn_recv,
    unit_ref,
    inv_ref,
    load_sem,
    tile_send,
    tile_recv,
    head_send,
    head_recv,
):
    me = lax.axis_index("tile")
    my_head = lax.axis_index("head")
    chips = n // 2
    chip, core = me // 2, lax.rem(me, 2)
    chans = qkv_ref.shape[1]
    wide = qkv_ref.shape[2]
    share_h = unit_ref.shape[0] // nh

    def at_tile(k):
        return (lax.rem(me + k, n), my_head)

    def at_chip(k):
        return (lax.rem(chip + k, chips) * 2 + core, my_head)

    partner = (chip * 2 + 1 - core, my_head)

    def at_head(k):
        return (me, lax.rem(my_head + k, nh))

    def send_tile(stage, k, src, dst, device):
        copy = pltpu.make_async_remote_copy(
            src_ref=src,
            dst_ref=dst,
            send_sem=tile_send.at[stage, k],
            recv_sem=tile_recv.at[stage, k],
            device_id=device,
            device_id_type=MESH,
        )
        copy.start()
        return copy

    def send_head(stage, k, src, dst, device):
        copy = pltpu.make_async_remote_copy(
            src_ref=src,
            dst_ref=dst,
            send_sem=head_send.at[stage, k],
            recv_sem=head_recv.at[stage, k],
            device_id=device,
            device_id_type=MESH,
        )
        copy.start()
        return copy

    started = []

    def arrived(copies):
        for copy in copies:
            copy.wait_recv()
        started.extend(copies)

    barrier = pltpu.get_barrier_semaphore()
    for k in range(1, n):
        pl.semaphore_signal(barrier, inc=1, device_id=at_tile(k), device_id_type=MESH)
    for k in range(1, nh):
        pl.semaphore_signal(barrier, inc=1, device_id=at_head(k), device_id_type=MESH)

    loads = {}
    for i, (name, src, dst) in enumerate(
        (
            ("cot", cot_hbm, cot_ref),
            ("tokens", tokens_hbm, tokens_ref),
            ("gain", gain_hbm, gain_ref),
            ("qkv", qkv_hbm, qkv_ref),
            ("kpool", kpool_hbm, kpool_ref),
            ("vpool", vpool_hbm, vpool_ref),
            ("qpool", qpool_hbm, qpool_ref),
            ("skip", skip_hbm, skip_ref),
            ("proj", proj_hbm, proj_ref),
        )
    ):
        loads[name] = pltpu.make_async_copy(src, dst, load_sem.at[i])
        loads[name].start()

    order = one_hot(token_order, TILE_H * TILE_W)
    loads["cot"].wait()
    cot_all[my_head] = cot_ref[...]
    pl.semaphore_wait(barrier, n + nh - 2)
    cot_copies = [
        send_head(0, k, cot_ref, cot_all.at[my_head], at_head(k)) for k in range(1, nh)
    ]

    loads["tokens"].wait()
    tokens = mm(order, tokens_ref[...])
    center = tokens - jnp.mean(tokens, axis=-1, keepdims=True)
    inv_std = lax.rsqrt(jnp.mean(center * center, axis=-1, keepdims=True) + EPSILON)
    unit = center * inv_std
    unit_ref[...] = unit
    inv_ref[...] = jnp.broadcast_to(inv_std, inv_ref.shape)
    loads["gain"].wait()
    gain = gain_ref[...].reshape(1, wide)
    normed = (unit * gain).astype(BF16)

    for name in ("qkv", "kpool", "vpool"):
        loads[name].wait()
    kpool = kpool_ref[...].astype(F32)
    vpool = vpool_ref[...].astype(F32)

    def pool_block(field, pool):
        total = pool[0:1] * field[0:SLAB]
        for s in range(1, 16):
            total = total + pool[s : s + 1] * field[s * SLAB : (s + 1) * SLAB]
        return total

    kv_all[0, 0:SLAB, :] = pool_block(mm(normed, qkv_ref[1], (1, 1)), kpool).astype(BF16)
    kv_all[1, 0:SLAB, :] = pool_block(mm(normed, qkv_ref[2], (1, 1)), vpool).astype(BF16)

    kv_copies = [
        send_tile(
            0,
            k,
            kv_all.at[:, 0:SLAB],
            kv_all.at[:, k * SLAB : (k + 1) * SLAB],
            at_tile(k),
        )
        for k in range(1, n)
    ]

    def cell_slabs(a, b):
        return [
            (2 * a2 + b2, (2 * a + a2) * 4 + 2 * b + b2) for a2 in range(2) for b2 in range(2)
        ]

    loads["qpool"].wait()
    qpool = qpool_ref[...].astype(F32)
    field = mm(normed, qkv_ref[0], (1, 1))
    query_parts = []
    input_parts = []
    for a in range(2):
        for b in range(2):
            total = None
            whole = None
            for w, s in cell_slabs(a, b):
                term = qpool[w : w + 1] * field[s * SLAB : (s + 1) * SLAB]
                total = term if total is None else total + term
                piece = tokens[s * SLAB : (s + 1) * SLAB]
                whole = piece if whole is None else whole + piece
            query_parts.append(total)
            input_parts.append(whole)
    queries_wide = jnp.concatenate(query_parts, axis=0).astype(BF16).astype(F32)
    pooled_input = (jnp.concatenate(input_parts, axis=0) * 0.25).astype(BF16)

    cells = one_hot(cell_order, CELLS)
    cells_back = one_hot(cell_order, CELLS, transposed=True)
    loads["skip"].wait()

    own_cot = mm(cells, cot_ref[...]).astype(BF16)
    d_pooled = mm(own_cot, skip_ref[...]).astype(BF16)
    half = CELLS // 2
    dp_send[0] = d_pooled[:half]
    dp_send[1] = d_pooled[half:]
    dp_copies = [
        send_head(
            1,
            k,
            dp_send.at[lax.rem(my_head + k, nh) * 2 // nh],
            dp_recv.at[k],
            at_head(k),
        )
        for k in range(1, nh)
    ]

    loads["proj"].wait()
    arrived(cot_copies)
    full_cot = jnp.concatenate([cot_all[h] for h in range(nh)], axis=1)
    full_cot = mm(cells, full_cot).astype(BF16)
    d_attended = mm(full_cot, proj_ref[...], (1, 1)).astype(BF16).astype(F32)

    heads = chans // HEAD_DIM
    lane = lax.broadcasted_iota(jnp.int32, (CELLS, chans), 1)
    masks = [
        jnp.logical_and(lane >= h * HEAD_DIM, lane < (h + 1) * HEAD_DIM) for h in range(heads)
    ]

    def by_head(x):
        return jnp.concatenate([jnp.where(m, x, 0.0) for m in masks], axis=0).astype(BF16)

    def from_heads(x):
        total = jnp.where(masks[0], x[:CELLS], 0.0)
        for h in range(1, heads):
            total = jnp.where(masks[h], x[h * CELLS : (h + 1) * CELLS], total)
        return total

    q_rows = by_head(queries_wide)
    g_rows = by_head(d_attended)

    arrived(kv_copies)
    keys = kv_all[0]
    values = kv_all[1]
    scale = HEAD_DIM ** (-0.5)
    exp_scores = jnp.exp(mm(keys, q_rows, (1, 1)) * scale)
    row_total = jnp.sum(exp_scores, axis=0, keepdims=True)
    probs = (exp_scores / row_total).astype(BF16)
    dprobs = mm(values, g_rows, (1, 1))
    probs_wide = probs.astype(F32)
    row_delta = jnp.sum(probs_wide * dprobs, axis=0, keepdims=True)
    d_scores = (scale * probs_wide * (dprobs - row_delta)).astype(BF16)
    key_grad = mm(d_scores, q_rows)
    value_grad = mm(probs, g_rows)
    kvg_send[0] = key_grad.astype(BF16)
    kvg_send[1] = value_grad.astype(BF16)
    kvg_copies = [
        send_tile(
            1,
            k,
            kvg_send.at[:, k * SLAB : (k + 1) * SLAB],
            kvg_recv.at[:, k * SLAB : (k + 1) * SLAB],
            at_tile(n - k),
        )
        for k in range(1, n)
    ]

    attended = (from_heads(mm(probs, values, (0, 0))) + queries_wide).astype(BF16)
    head_part = mm(mm(cells_back, attended).astype(BF16), proj_ref[...])
    for h in range(nh):
        hp_send[h] = head_part[:, h * chans : (h + 1) * chans].astype(BF16)
    hp_copies = [
        send_head(2, k, hp_send.at[lax.rem(my_head + k, nh)], hp_recv.at[k], at_head(k))
        for k in range(1, nh)
    ]

    query_grad = from_heads(mm(d_scores, keys, (0, 0))) + d_attended
    spread = []
    for s in range(16):
        a, b = s // 4, s % 4
        cell = (a // 2) * 2 + b // 2
        w = (a % 2) * 2 + b % 2
        spread.append(qpool[w : w + 1] * query_grad[cell * SLAB : (cell + 1) * SLAB])
    d_projected = jnp.concatenate(spread, axis=0).astype(BF16)
    ga_send[0:chans, :] = mm(d_projected, normed, (0, 0)).astype(BF16)
    proj_part = mm(attended, full_cot, (0, 0)).astype(BF16)
    halves = proj_part.shape[1] // wide
    for i in range(halves):
        ga_send[(i + 1) * chans : (i + 2) * chans, :] = proj_part[:, i * wide : (i + 1) * wide]
    filled = (halves + 1) * chans
    if ga_send.shape[0] > filled:
        ga_send[filled:, :] = jnp.zeros((ga_send.shape[0] - filled, wide), BF16)
    half_a = chips * share_a
    ga_pairs = [
        send_tile(2, 1, ga_send.at[rows((1 - core) * half_a, half_a)], ga_pair, partner)
    ]
    d_normed = mm(d_projected, qkv_ref[0])

    def fold(stage, pairs, sent, pair, part, received, share):
        arrived(pairs)
        size = chips * share
        total = sent[rows(core * size, size), :].astype(F32) + pair[...].astype(F32)
        part[...] = total.astype(BF16)
        return [
            send_tile(
                stage,
                k,
                part.at[rows(lax.rem(chip + k, chips) * share, share)],
                received.at[k],
                at_chip(k),
            )
            for k in range(1, chips)
        ]

    def place(k, share):
        from_chip = lax.rem(chip + chips - k, chips)
        return rows((core * chips + from_chip) * share, share)

    def reduce_and_share(stage, copies, part, received, out, share):
        arrived(copies)
        total = part[rows(chip * share, share), :].astype(F32)
        for k in range(1, chips):
            total = total + received[k].astype(F32)
        mine = place(0, share)
        out[mine, :] = total.astype(BF16)
        shares = [
            send_tile(stage, k, out.at[mine], out.at[mine], at_chip(k))
            for k in range(1, chips)
        ]
        relays = [send_tile(stage + 1, 0, out.at[mine], out.at[mine], partner)]
        return shares, relays

    def relay(stage, shares, relays, out, share):
        for k in range(1, chips):
            arrived(shares[k - 1 : k])
            there = place(k, share)
            relays.append(send_tile(stage, k, out.at[there], out.at[there], partner))

    ga_copies = fold(3, ga_pairs, ga_send, ga_pair, ga_part, ga_recv, share_a)

    arrived(kvg_copies)
    d_fields = []
    for j, pool, own in ((0, kpool, key_grad), (1, vpool, value_grad)):
        total = own[0:SLAB]
        for k in range(1, n):
            total = total + kvg_recv[j, k * SLAB : (k + 1) * SLAB, :].astype(F32)
        d_projected = jnp.concatenate([pool[s : s + 1] * total for s in range(16)], axis=0)
        d_fields.append(d_projected.astype(BF16))
        d_normed = d_normed + mm(d_fields[j], qkv_ref[j + 1])
    dn_send[...] = d_normed.astype(BF16)
    piece = share_h // 2
    dn_copies = [
        [
            send_head(
                3 + half,
                k,
                dn_send.at[rows(lax.rem(my_head + k, nh) * share_h + half * piece, piece)],
                dn_recv.at[k, half * piece : (half + 1) * piece],
                at_head(k),
            )
            for k in range(1, nh)
        ]
        for half in range(2)
    ]
    for j in range(2):
        gb_send[j * chans : (j + 1) * chans, :] = mm(d_fields[j], normed, (0, 0)).astype(BF16)
    filled = 2 * chans
    if gb_send.shape[0] > filled:
        gb_send[filled:, :] = jnp.zeros((gb_send.shape[0] - filled, wide), BF16)
    gb_copies = [
        send_tile(
            6,
            k,
            gb_send.at[rows(lax.rem(me + k, n) * share_b, share_b)],
            gb_recv.at[k],
            at_tile(k),
        )
        for k in range(1, n)
    ]

    pooled_input = mm(cells_back, pooled_input).astype(BF16)
    skipped = mm(pooled_input, skip_ref[...], (1, 1))
    arrived(dp_copies)
    d_pooled = dp_send[my_head * 2 // nh].astype(F32)
    for k in range(1, nh):
        d_pooled = d_pooled + dp_recv[k].astype(F32)
    d_pooled = d_pooled * 0.25

    ga_shares, ga_relays = reduce_and_share(4, ga_copies, ga_part, ga_recv, ga_out, share_a)

    arrived(hp_copies)
    summed = hp_send[my_head].astype(F32)
    for k in range(1, nh):
        summed = summed + hp_recv[k].astype(F32)
    block_out_ref[...] = (summed + skipped).astype(BF16)

    def share_input(half):
        arrived(dn_copies[half])
        mine = rows(my_head * share_h + half * piece, piece)
        d_normed = dn_send[mine, :].astype(F32)
        for k in range(1, nh):
            d_normed = d_normed + dn_recv[k, half * piece : (half + 1) * piece, :].astype(F32)
        scaled = d_normed * gain
        own_unit = unit_ref[mine, :]
        back = inv_ref[mine, :][:, 0:1] * (
            scaled
            - jnp.mean(scaled, axis=-1, keepdims=True)
            - own_unit * jnp.mean(scaled * own_unit, axis=-1, keepdims=True)
        )
        cell = d_pooled[half * SLAB : (half + 1) * SLAB]
        ig_all[mine, :] = (back + jnp.concatenate([cell, cell], axis=0)).astype(BF16)
        return [
            send_head(5 + half, k, ig_all.at[mine], ig_all.at[mine], at_head(k))
            for k in range(1, nh)
        ]

    ig_copies = share_input(0)
    arrived(gb_copies)
    mine = rows(me * share_b, share_b)
    total = gb_send[mine, :].astype(F32)
    for k in range(1, n):
        total = total + gb_recv[k].astype(F32)
    gb_out[mine, :] = total.astype(BF16)
    gb_shares = [
        send_tile(7, k, gb_out.at[mine], gb_out.at[mine], at_tile(k)) for k in range(1, n)
    ]
    ig_copies += share_input(1)
    relay(5, ga_shares, ga_relays, ga_out, share_a)
    arrived(ig_copies)
    arrived(ga_relays)
    arrived(gb_shares)
    for copy in started:
        copy.wait_send()


def finish(
    block_ref, ig_ref, ga_ref, gb_ref, block_hbm, ig_hbm, qkv_hbm, proj_hbm, ig, qkv, proj, sems
):
    chans, wide = qkv.shape[1:]
    copies = []

    def put(src, dst):
        copy = pltpu.make_async_copy(src, dst, sems.at[len(copies)])
        copy.start()
        copies.append(copy)

    back = one_hot(token_order, TILE_H * TILE_W, transposed=True)
    ig[...] = mm(back, ig_ref[...]).astype(BF16)
    put(ig, ig_hbm)
    put(block_ref, block_hbm)
    for i in range(proj.shape[1] // wide):
        proj[:, i * wide : (i + 1) * wide] = ga_ref[
            (i + 1) * chans : (i + 2) * chans, :
        ].astype(F32)
    put(proj, proj_hbm)
    for j, part in enumerate(
        (ga_ref[0:chans, :], gb_ref[0:chans, :], gb_ref[chans : 2 * chans, :])
    ):
        qkv[j] = part.astype(F32)
        put(qkv.at[j], qkv_hbm.at[j])
    for copy in copies:
        copy.wait()


def share_of(total, n):
    return -(-total // (n * 16)) * 16


def local(n, nh, *operands):
    tokens, ln_gain, qkv, qpool, kpool, vpool, proj, skip, cot = operands
    count, wide = tokens.shape
    chans = qkv.shape[1]
    full = proj.shape[1]
    share_a = share_of(chans * (1 + full // wide), n)
    share_b = share_of(chans * 2, n)
    share_h = count // nh
    vmem = pl.BlockSpec(memory_space=pltpu.VMEM)
    hbm = pl.BlockSpec(memory_space=pltpu.HBM)
    outs = pl.pallas_call(
        functools.partial(kernel, n, nh, share_a, share_b),
        out_shape=(
            jax.ShapeDtypeStruct(cot.shape, BF16),
            jax.ShapeDtypeStruct(tokens.shape, BF16),
            jax.ShapeDtypeStruct((n * share_a, wide), BF16),
            jax.ShapeDtypeStruct((n * share_b, wide), BF16),
        ),
        in_specs=[hbm] * 9,
        out_specs=(vmem,) * 4,
        scratch_shapes=[pltpu.VMEM(x.shape, x.dtype) for x in operands]
        + [
            pltpu.VMEM((nh,) + cot.shape, BF16),
            pltpu.VMEM((2, n * SLAB, chans), BF16),
            pltpu.VMEM((2, n * SLAB, chans), BF16),
            pltpu.VMEM((2, n * SLAB, chans), BF16),
            pltpu.VMEM((2, CELLS // 2, wide), BF16),
            pltpu.VMEM((nh, CELLS // 2, wide), BF16),
            pltpu.VMEM((nh,) + cot.shape, BF16),
            pltpu.VMEM((nh,) + cot.shape, BF16),
            pltpu.VMEM((n * share_a, wide), BF16),
            pltpu.VMEM((n // 2 * share_a, wide), BF16),
            pltpu.VMEM((n // 2 * share_a, wide), BF16),
            pltpu.VMEM((n // 2, share_a, wide), BF16),
            pltpu.VMEM((n * share_b, wide), BF16),
            pltpu.VMEM((n, share_b, wide), BF16),
            pltpu.VMEM((count, wide), BF16),
            pltpu.VMEM((nh, share_h, wide), BF16),
            pltpu.VMEM((count, wide), F32),
            pltpu.VMEM((count, 128), F32),
            pltpu.SemaphoreType.DMA((9,)),
            pltpu.SemaphoreType.DMA((8, n)),
            pltpu.SemaphoreType.DMA((8, n)),
            pltpu.SemaphoreType.DMA((7, nh)),
            pltpu.SemaphoreType.DMA((7, nh)),
        ],
        compiler_params=pltpu.CompilerParams(
            collective_id=0, has_side_effects=True, vmem_limit_bytes=40 * 1024 * 1024
        ),
    )(*[pltpu.with_memory_space_constraint(x, pltpu.HBM) for x in operands])
    return pl.pallas_call(
        finish,
        out_shape=(
            jax.ShapeDtypeStruct(cot.shape, BF16),
            jax.ShapeDtypeStruct(tokens.shape, BF16),
            jax.ShapeDtypeStruct(qkv.shape, F32),
            jax.ShapeDtypeStruct(proj.shape, F32),
        ),
        in_specs=[vmem] * 4,
        out_specs=(hbm,) * 4,
        scratch_shapes=[
            pltpu.VMEM(tokens.shape, BF16),
            pltpu.VMEM(qkv.shape, F32),
            pltpu.VMEM(proj.shape, F32),
            pltpu.SemaphoreType.DMA((6,)),
        ],
        compiler_params=pltpu.CompilerParams(vmem_limit_bytes=16 * 1024 * 1024),
    )(*outs)


def solution(mesh):
    placed = (
        P("tile", None),
        P(),
        P(None, "head", None),
        P(None, "head"),
        P(None, "head"),
        P(None, "head"),
        P("head", None),
        P("head", None),
        P("tile", "head"),
    )
    return jax.shard_map(
        functools.partial(local, mesh.shape["tile"], mesh.shape["head"]),
        mesh=mesh,
        in_specs=placed,
        out_specs=(P("tile", "head"), P("tile", None), P(None, "head", None), P("head", None)),
        check_vma=False,
    )
```

```python
import functools

import jax
import jax.numpy as jnp
from jax import lax
from jax.experimental import pallas as pl
from jax.experimental.pallas import tpu as pltpu
from jax.sharding import PartitionSpec as P

HEAD_DIM = 96
TILE_H = 8
TILE_W = 32
EPSILON = 1e-06
SLAB = TILE_H * TILE_W // 16
CELLS = SLAB * 4
MESH = pl.DeviceIdType.MESH
F32 = jnp.float32
BF16 = jnp.bfloat16


def mm(a, b, contract=(1, 0)):
    return lax.dot_general(
        a, b, (((contract[0],), (contract[1],)), ((), ())), preferred_element_type=F32
    )


def token_order(shape, dim):
    p = lax.broadcasted_iota(jnp.int32, shape, dim)
    slab, block = p >> 4, p & 15
    a, b = slab >> 2, slab & 3
    return ((block >> 3) * 4 + a) * TILE_W + (block & 7) * 4 + b


def cell_order(shape, dim):
    p = lax.broadcasted_iota(jnp.int32, shape, dim)
    slab, block = p >> 4, p & 15
    a, b = slab >> 1, slab & 1
    return ((block >> 3) * 2 + a) * (TILE_W // 2) + (block & 7) * 2 + b


def one_hot(order, size, transposed=False):
    shape = (size, size)
    dim = 1 if transposed else 0
    other = lax.broadcasted_iota(jnp.int32, shape, 1 - dim)
    return jnp.where(order(shape, dim) == other, 1.0, 0.0).astype(BF16)


def rows(start, size):
    return pl.ds(pl.multiple_of(start, 16), size)


def kernel(
    n,
    nh,
    share_a,
    share_b,
    tokens_hbm,
    gain_hbm,
    qkv_hbm,
    qpool_hbm,
    kpool_hbm,
    vpool_hbm,
    proj_hbm,
    skip_hbm,
    cot_hbm,
    block_out_ref,
    ig_all,
    ga_out,
    gb_out,
    tokens_ref,
    gain_ref,
    qkv_ref,
    qpool_ref,
    kpool_ref,
    vpool_ref,
    proj_ref,
    skip_ref,
    cot_ref,
    cot_all,
    kv_all,
    kvg_send,
    kvg_recv,
    dp_send,
    dp_recv,
    hp_send,
    hp_recv,
    ga_send,
    ga_pair,
    ga_part,
    ga_recv,
    gb_send,
    gb_recv,
    dn_send,
    dn_recv,
    unit_ref,
    inv_ref,
    load_sem,
    tile_send,
    tile_recv,
    head_send,
    head_recv,
):
    me = lax.axis_index("tile")
    my_head = lax.axis_index("head")
    chips = n // 2
    chip, core = me // 2, lax.rem(me, 2)
    chans = qkv_ref.shape[1]
    wide = qkv_ref.shape[2]
    share_h = unit_ref.shape[0] // nh

    def at_tile(k):
        return (lax.rem(me + k, n), my_head)

    def at_chip(k):
        return (lax.rem(chip + k, chips) * 2 + core, my_head)

    partner = (chip * 2 + 1 - core, my_head)

    def at_head(k):
        return (me, lax.rem(my_head + k, nh))

    def send_tile(stage, k, src, dst, device):
        copy = pltpu.make_async_remote_copy(
            src_ref=src,
            dst_ref=dst,
            send_sem=tile_send.at[stage, k],
            recv_sem=tile_recv.at[stage, k],
            device_id=device,
            device_id_type=MESH,
        )
        copy.start()
        return copy

    def send_head(stage, k, src, dst, device):
        copy = pltpu.make_async_remote_copy(
            src_ref=src,
            dst_ref=dst,
            send_sem=head_send.at[stage, k],
            recv_sem=head_recv.at[stage, k],
            device_id=device,
            device_id_type=MESH,
        )
        copy.start()
        return copy

    started = []

    def arrived(copies):
        for copy in copies:
            copy.wait_recv()
        started.extend(copies)

    barrier = pltpu.get_barrier_semaphore()
    for k in range(1, n):
        pl.semaphore_signal(barrier, inc=1, device_id=at_tile(k), device_id_type=MESH)
    for k in range(1, nh):
        pl.semaphore_signal(barrier, inc=1, device_id=at_head(k), device_id_type=MESH)

    loads = {}
    for i, (name, src, dst) in enumerate(
        (
            ("cot", cot_hbm, cot_ref),
            ("tokens", tokens_hbm, tokens_ref),
            ("gain", gain_hbm, gain_ref),
            ("qkv", qkv_hbm, qkv_ref),
            ("kpool", kpool_hbm, kpool_ref),
            ("vpool", vpool_hbm, vpool_ref),
            ("qpool", qpool_hbm, qpool_ref),
            ("skip", skip_hbm, skip_ref),
            ("proj", proj_hbm, proj_ref),
        )
    ):
        loads[name] = pltpu.make_async_copy(src, dst, load_sem.at[i])
        loads[name].start()

    order = one_hot(token_order, TILE_H * TILE_W)
    loads["cot"].wait()
    cot_all[my_head] = cot_ref[...]
    pl.semaphore_wait(barrier, n + nh - 2)
    cot_copies = [
        send_head(0, k, cot_ref, cot_all.at[my_head], at_head(k)) for k in range(1, nh)
    ]

    loads["tokens"].wait()
    tokens = mm(order, tokens_ref[...])
    center = tokens - jnp.mean(tokens, axis=-1, keepdims=True)
    inv_std = lax.rsqrt(jnp.mean(center * center, axis=-1, keepdims=True) + EPSILON)
    unit = center * inv_std
    unit_ref[...] = unit
    inv_ref[...] = jnp.broadcast_to(inv_std, inv_ref.shape)
    loads["gain"].wait()
    gain = gain_ref[...].reshape(1, wide)
    normed = (unit * gain).astype(BF16)

    for name in ("qkv", "kpool", "vpool"):
        loads[name].wait()
    kpool = kpool_ref[...].astype(F32)
    vpool = vpool_ref[...].astype(F32)

    def pool_block(field, pool):
        total = pool[0:1] * field[0:SLAB]
        for s in range(1, 16):
            total = total + pool[s : s + 1] * field[s * SLAB : (s + 1) * SLAB]
        return total

    kv_all[0, 0:SLAB, :] = pool_block(mm(normed, qkv_ref[1], (1, 1)), kpool).astype(BF16)
    kv_all[1, 0:SLAB, :] = pool_block(mm(normed, qkv_ref[2], (1, 1)), vpool).astype(BF16)

    kv_copies = [
        send_tile(
            0,
            k,
            kv_all.at[:, 0:SLAB],
            kv_all.at[:, k * SLAB : (k + 1) * SLAB],
            at_tile(k),
        )
        for k in range(1, n)
    ]

    def cell_slabs(a, b):
        return [
            (2 * a2 + b2, (2 * a + a2) * 4 + 2 * b + b2) for a2 in range(2) for b2 in range(2)
        ]

    loads["qpool"].wait()
    qpool = qpool_ref[...].astype(F32)
    field = mm(normed, qkv_ref[0], (1, 1))
    query_parts = []
    input_parts = []
    for a in range(2):
        for b in range(2):
            total = None
            whole = None
            for w, s in cell_slabs(a, b):
                term = qpool[w : w + 1] * field[s * SLAB : (s + 1) * SLAB]
                total = term if total is None else total + term
                piece = tokens[s * SLAB : (s + 1) * SLAB]
                whole = piece if whole is None else whole + piece
            query_parts.append(total)
            input_parts.append(whole)
    queries_wide = jnp.concatenate(query_parts, axis=0).astype(BF16).astype(F32)
    pooled_input = (jnp.concatenate(input_parts, axis=0) * 0.25).astype(BF16)

    cells = one_hot(cell_order, CELLS)
    cells_back = one_hot(cell_order, CELLS, transposed=True)
    loads["skip"].wait()

    own_cot = mm(cells, cot_ref[...]).astype(BF16)
    d_pooled = mm(own_cot, skip_ref[...]).astype(BF16)
    half = CELLS // 2
    dp_send[0] = d_pooled[:half]
    dp_send[1] = d_pooled[half:]
    dp_copies = [
        send_head(
            1,
            k,
            dp_send.at[lax.rem(my_head + k, nh) * 2 // nh],
            dp_recv.at[k],
            at_head(k),
        )
        for k in range(1, nh)
    ]

    loads["proj"].wait()
    arrived(cot_copies)
    full_cot = jnp.concatenate([cot_all[h] for h in range(nh)], axis=1)
    full_cot = mm(cells, full_cot).astype(BF16)
    d_attended = mm(full_cot, proj_ref[...], (1, 1)).astype(BF16).astype(F32)

    heads = chans // HEAD_DIM
    lane = lax.broadcasted_iota(jnp.int32, (CELLS, chans), 1)
    masks = [
        jnp.logical_and(lane >= h * HEAD_DIM, lane < (h + 1) * HEAD_DIM) for h in range(heads)
    ]

    def by_head(x):
        return jnp.concatenate([jnp.where(m, x, 0.0) for m in masks], axis=0).astype(BF16)

    def from_heads(x):
        total = jnp.where(masks[0], x[:CELLS], 0.0)
        for h in range(1, heads):
            total = jnp.where(masks[h], x[h * CELLS : (h + 1) * CELLS], total)
        return total

    q_rows = by_head(queries_wide)
    g_rows = by_head(d_attended)

    arrived(kv_copies)
    keys = kv_all[0]
    values = kv_all[1]
    scale = HEAD_DIM ** (-0.5)
    exp_scores = jnp.exp(mm(keys, q_rows, (1, 1)) * scale)
    row_total = jnp.sum(exp_scores, axis=0, keepdims=True)
    probs = (exp_scores / row_total).astype(BF16)
    dprobs = mm(values, g_rows, (1, 1))
    probs_wide = probs.astype(F32)
    row_delta = jnp.sum(probs_wide * dprobs, axis=0, keepdims=True)
    d_scores = (scale * probs_wide * (dprobs - row_delta)).astype(BF16)
    key_grad = mm(d_scores, q_rows)
    value_grad = mm(probs, g_rows)
    kvg_send[0] = key_grad.astype(BF16)
    kvg_send[1] = value_grad.astype(BF16)
    kvg_copies = [
        send_tile(
            1,
            k,
            kvg_send.at[:, k * SLAB : (k + 1) * SLAB],
            kvg_recv.at[:, k * SLAB : (k + 1) * SLAB],
            at_tile(n - k),
        )
        for k in range(1, n)
    ]

    attended = (from_heads(mm(probs, values, (0, 0))) + queries_wide).astype(BF16)
    head_part = mm(mm(cells_back, attended).astype(BF16), proj_ref[...])
    for h in range(nh):
        hp_send[h] = head_part[:, h * chans : (h + 1) * chans].astype(BF16)
    hp_copies = [
        send_head(2, k, hp_send.at[lax.rem(my_head + k, nh)], hp_recv.at[k], at_head(k))
        for k in range(1, nh)
    ]

    query_grad = from_heads(mm(d_scores, keys, (0, 0))) + d_attended
    spread = []
    for s in range(16):
        a, b = s // 4, s % 4
        cell = (a // 2) * 2 + b // 2
        w = (a % 2) * 2 + b % 2
        spread.append(qpool[w : w + 1] * query_grad[cell * SLAB : (cell + 1) * SLAB])
    d_projected = jnp.concatenate(spread, axis=0).astype(BF16)
    ga_send[0:chans, :] = mm(d_projected, normed, (0, 0)).astype(BF16)
    proj_part = mm(attended, full_cot, (0, 0)).astype(BF16)
    halves = proj_part.shape[1] // wide
    for i in range(halves):
        ga_send[(i + 1) * chans : (i + 2) * chans, :] = proj_part[:, i * wide : (i + 1) * wide]
    filled = (halves + 1) * chans
    if ga_send.shape[0] > filled:
        ga_send[filled:, :] = jnp.zeros((ga_send.shape[0] - filled, wide), BF16)
    half_a = chips * share_a
    ga_pairs = [
        send_tile(2, 1, ga_send.at[rows((1 - core) * half_a, half_a)], ga_pair, partner)
    ]
    d_normed = mm(d_projected, qkv_ref[0])

    def fold(stage, pairs, sent, pair, part, received, share):
        arrived(pairs)
        size = chips * share
        total = sent[rows(core * size, size), :].astype(F32) + pair[...].astype(F32)
        part[...] = total.astype(BF16)
        return [
            send_tile(
                stage,
                k,
                part.at[rows(lax.rem(chip + k, chips) * share, share)],
                received.at[k],
                at_chip(k),
            )
            for k in range(1, chips)
        ]

    def place(k, share):
        from_chip = lax.rem(chip + chips - k, chips)
        return rows((core * chips + from_chip) * share, share)

    def reduce_and_share(stage, copies, part, received, out, share):
        arrived(copies)
        total = part[rows(chip * share, share), :].astype(F32)
        for k in range(1, chips):
            total = total + received[k].astype(F32)
        mine = place(0, share)
        out[mine, :] = total.astype(BF16)
        shares = [
            send_tile(stage, k, out.at[mine], out.at[mine], at_chip(k))
            for k in range(1, chips)
        ]
        relays = [send_tile(stage + 1, 0, out.at[mine], out.at[mine], partner)]
        return shares, relays

    def relay(stage, shares, relays, out, share):
        for k in range(1, chips):
            arrived(shares[k - 1 : k])
            there = place(k, share)
            relays.append(send_tile(stage, k, out.at[there], out.at[there], partner))

    arrived(kvg_copies)
    d_fields = []
    for j, pool, own in ((0, kpool, key_grad), (1, vpool, value_grad)):
        total = own[0:SLAB]
        for k in range(1, n):
            total = total + kvg_recv[j, k * SLAB : (k + 1) * SLAB, :].astype(F32)
        d_projected = jnp.concatenate([pool[s : s + 1] * total for s in range(16)], axis=0)
        d_fields.append(d_projected.astype(BF16))
        d_normed = d_normed + mm(d_fields[j], qkv_ref[j + 1])
    dn_send[...] = d_normed.astype(BF16)
    piece = share_h // 2
    dn_copies = [
        [
            send_head(
                3 + half,
                k,
                dn_send.at[rows(lax.rem(my_head + k, nh) * share_h + half * piece, piece)],
                dn_recv.at[k, half * piece : (half + 1) * piece],
                at_head(k),
            )
            for k in range(1, nh)
        ]
        for half in range(2)
    ]
    ga_copies = fold(3, ga_pairs, ga_send, ga_pair, ga_part, ga_recv, share_a)
    for j in range(2):
        gb_send[j * chans : (j + 1) * chans, :] = mm(d_fields[j], normed, (0, 0)).astype(BF16)
    filled = 2 * chans
    if gb_send.shape[0] > filled:
        gb_send[filled:, :] = jnp.zeros((gb_send.shape[0] - filled, wide), BF16)
    gb_copies = [
        send_tile(
            6,
            k,
            gb_send.at[rows(lax.rem(me + k, n) * share_b, share_b)],
            gb_recv.at[k],
            at_tile(k),
        )
        for k in range(1, n)
    ]

    pooled_input = mm(cells_back, pooled_input).astype(BF16)
    skipped = mm(pooled_input, skip_ref[...], (1, 1))
    arrived(dp_copies)
    d_pooled = dp_send[my_head * 2 // nh].astype(F32)
    for k in range(1, nh):
        d_pooled = d_pooled + dp_recv[k].astype(F32)
    d_pooled = d_pooled * 0.25


    def share_input(half):
        arrived(dn_copies[half])
        mine = rows(my_head * share_h + half * piece, piece)
        d_normed = dn_send[mine, :].astype(F32)
        for k in range(1, nh):
            d_normed = d_normed + dn_recv[k, half * piece : (half + 1) * piece, :].astype(F32)
        scaled = d_normed * gain
        own_unit = unit_ref[mine, :]
        back = inv_ref[mine, :][:, 0:1] * (
            scaled
            - jnp.mean(scaled, axis=-1, keepdims=True)
            - own_unit * jnp.mean(scaled * own_unit, axis=-1, keepdims=True)
        )
        cell = d_pooled[half * SLAB : (half + 1) * SLAB]
        ig_all[mine, :] = (back + jnp.concatenate([cell, cell], axis=0)).astype(BF16)
        return [
            send_head(5 + half, k, ig_all.at[mine], ig_all.at[mine], at_head(k))
            for k in range(1, nh)
        ]

    ig_copies = share_input(0)
    ga_shares, ga_relays = reduce_and_share(4, ga_copies, ga_part, ga_recv, ga_out, share_a)
    ig_copies += share_input(1)
    arrived(gb_copies)
    mine = rows(me * share_b, share_b)
    total = gb_send[mine, :].astype(F32)
    for k in range(1, n):
        total = total + gb_recv[k].astype(F32)
    gb_out[mine, :] = total.astype(BF16)
    gb_shares = [
        send_tile(7, k, gb_out.at[mine], gb_out.at[mine], at_tile(k)) for k in range(1, n)
    ]
    arrived(hp_copies)
    summed = hp_send[my_head].astype(F32)
    for k in range(1, nh):
        summed = summed + hp_recv[k].astype(F32)
    block_out_ref[...] = (summed + skipped).astype(BF16)

    relay(5, ga_shares, ga_relays, ga_out, share_a)
    arrived(ig_copies)
    arrived(ga_relays)
    arrived(gb_shares)
    for copy in started:
        copy.wait_send()


def finish(
    block_ref, ig_ref, ga_ref, gb_ref, block_hbm, ig_hbm, qkv_hbm, proj_hbm, ig, qkv, proj, sems
):
    chans, wide = qkv.shape[1:]
    copies = []

    def put(src, dst):
        copy = pltpu.make_async_copy(src, dst, sems.at[len(copies)])
        copy.start()
        copies.append(copy)

    back = one_hot(token_order, TILE_H * TILE_W, transposed=True)
    ig[...] = mm(back, ig_ref[...]).astype(BF16)
    put(ig, ig_hbm)
    put(block_ref, block_hbm)
    for i in range(proj.shape[1] // wide):
        proj[:, i * wide : (i + 1) * wide] = ga_ref[
            (i + 1) * chans : (i + 2) * chans, :
        ].astype(F32)
    put(proj, proj_hbm)
    for j, part in enumerate(
        (ga_ref[0:chans, :], gb_ref[0:chans, :], gb_ref[chans : 2 * chans, :])
    ):
        qkv[j] = part.astype(F32)
        put(qkv.at[j], qkv_hbm.at[j])
    for copy in copies:
        copy.wait()


def share_of(total, n):
    return -(-total // (n * 16)) * 16


def local(n, nh, *operands):
    tokens, ln_gain, qkv, qpool, kpool, vpool, proj, skip, cot = operands
    count, wide = tokens.shape
    chans = qkv.shape[1]
    full = proj.shape[1]
    share_a = share_of(chans * (1 + full // wide), n)
    share_b = share_of(chans * 2, n)
    share_h = count // nh
    vmem = pl.BlockSpec(memory_space=pltpu.VMEM)
    hbm = pl.BlockSpec(memory_space=pltpu.HBM)
    outs = pl.pallas_call(
        functools.partial(kernel, n, nh, share_a, share_b),
        out_shape=(
            jax.ShapeDtypeStruct(cot.shape, BF16),
            jax.ShapeDtypeStruct(tokens.shape, BF16),
            jax.ShapeDtypeStruct((n * share_a, wide), BF16),
            jax.ShapeDtypeStruct((n * share_b, wide), BF16),
        ),
        in_specs=[hbm] * 9,
        out_specs=(vmem,) * 4,
        scratch_shapes=[pltpu.VMEM(x.shape, x.dtype) for x in operands]
        + [
            pltpu.VMEM((nh,) + cot.shape, BF16),
            pltpu.VMEM((2, n * SLAB, chans), BF16),
            pltpu.VMEM((2, n * SLAB, chans), BF16),
            pltpu.VMEM((2, n * SLAB, chans), BF16),
            pltpu.VMEM((2, CELLS // 2, wide), BF16),
            pltpu.VMEM((nh, CELLS // 2, wide), BF16),
            pltpu.VMEM((nh,) + cot.shape, BF16),
            pltpu.VMEM((nh,) + cot.shape, BF16),
            pltpu.VMEM((n * share_a, wide), BF16),
            pltpu.VMEM((n // 2 * share_a, wide), BF16),
            pltpu.VMEM((n // 2 * share_a, wide), BF16),
            pltpu.VMEM((n // 2, share_a, wide), BF16),
            pltpu.VMEM((n * share_b, wide), BF16),
            pltpu.VMEM((n, share_b, wide), BF16),
            pltpu.VMEM((count, wide), BF16),
            pltpu.VMEM((nh, share_h, wide), BF16),
            pltpu.VMEM((count, wide), F32),
            pltpu.VMEM((count, 128), F32),
            pltpu.SemaphoreType.DMA((9,)),
            pltpu.SemaphoreType.DMA((8, n)),
            pltpu.SemaphoreType.DMA((8, n)),
            pltpu.SemaphoreType.DMA((7, nh)),
            pltpu.SemaphoreType.DMA((7, nh)),
        ],
        compiler_params=pltpu.CompilerParams(
            collective_id=0, has_side_effects=True, vmem_limit_bytes=40 * 1024 * 1024
        ),
    )(*[pltpu.with_memory_space_constraint(x, pltpu.HBM) for x in operands])
    return pl.pallas_call(
        finish,
        out_shape=(
            jax.ShapeDtypeStruct(cot.shape, BF16),
            jax.ShapeDtypeStruct(tokens.shape, BF16),
            jax.ShapeDtypeStruct(qkv.shape, F32),
            jax.ShapeDtypeStruct(proj.shape, F32),
        ),
        in_specs=[vmem] * 4,
        out_specs=(hbm,) * 4,
        scratch_shapes=[
            pltpu.VMEM(tokens.shape, BF16),
            pltpu.VMEM(qkv.shape, F32),
            pltpu.VMEM(proj.shape, F32),
            pltpu.SemaphoreType.DMA((6,)),
        ],
        compiler_params=pltpu.CompilerParams(vmem_limit_bytes=16 * 1024 * 1024),
    )(*outs)


def solution(mesh):
    placed = (
        P("tile", None),
        P(),
        P(None, "head", None),
        P(None, "head"),
        P(None, "head"),
        P(None, "head"),
        P("head", None),
        P("head", None),
        P("tile", "head"),
    )
    return jax.shard_map(
        functools.partial(local, mesh.shape["tile"], mesh.shape["head"]),
        mesh=mesh,
        in_specs=placed,
        out_specs=(P("tile", "head"), P("tile", None), P(None, "head", None), P("head", None)),
        check_vma=False,
    )
```

```python
import functools

import jax
import jax.numpy as jnp
from jax import lax
from jax.experimental import pallas as pl
from jax.experimental.pallas import tpu as pltpu
from jax.sharding import PartitionSpec as P

HEAD_DIM = 96
TILE_H = 8
TILE_W = 32
EPSILON = 1e-06
SLAB = TILE_H * TILE_W // 16
CELLS = SLAB * 4
MESH = pl.DeviceIdType.MESH
F32 = jnp.float32
BF16 = jnp.bfloat16


def mm(a, b, contract=(1, 0)):
    return lax.dot_general(
        a, b, (((contract[0],), (contract[1],)), ((), ())), preferred_element_type=F32
    )


def token_order(shape, dim):
    p = lax.broadcasted_iota(jnp.int32, shape, dim)
    slab, block = p >> 4, p & 15
    a, b = slab >> 2, slab & 3
    return ((block >> 3) * 4 + a) * TILE_W + (block & 7) * 4 + b


def cell_order(shape, dim):
    p = lax.broadcasted_iota(jnp.int32, shape, dim)
    slab, block = p >> 4, p & 15
    a, b = slab >> 1, slab & 1
    return ((block >> 3) * 2 + a) * (TILE_W // 2) + (block & 7) * 2 + b


def one_hot(order, size, transposed=False):
    shape = (size, size)
    dim = 1 if transposed else 0
    other = lax.broadcasted_iota(jnp.int32, shape, 1 - dim)
    return jnp.where(order(shape, dim) == other, 1.0, 0.0).astype(BF16)


def rows(start, size):
    return pl.ds(pl.multiple_of(start, 16), size)


def kernel(
    n,
    nh,
    share_a,
    share_b,
    tokens_hbm,
    gain_hbm,
    qkv_hbm,
    qpool_hbm,
    kpool_hbm,
    vpool_hbm,
    proj_hbm,
    skip_hbm,
    cot_hbm,
    block_out_ref,
    ig_all,
    ga_out,
    gb_out,
    tokens_ref,
    gain_ref,
    qkv_ref,
    qpool_ref,
    kpool_ref,
    vpool_ref,
    proj_ref,
    skip_ref,
    cot_ref,
    cot_all,
    kv_all,
    kvg_send,
    kvg_recv,
    dp_send,
    dp_recv,
    hp_send,
    hp_recv,
    ga_send,
    ga_pair,
    ga_part,
    ga_recv,
    gb_send,
    gb_pair,
    gb_part,
    gb_recv,
    dn_send,
    dn_recv,
    unit_ref,
    inv_ref,
    load_sem,
    tile_send,
    tile_recv,
    head_send,
    head_recv,
):
    me = lax.axis_index("tile")
    my_head = lax.axis_index("head")
    chips = n // 2
    chip, core = me // 2, lax.rem(me, 2)
    chans = qkv_ref.shape[1]
    wide = qkv_ref.shape[2]
    share_h = unit_ref.shape[0] // nh

    def at_tile(k):
        return (lax.rem(me + k, n), my_head)

    def at_chip(k):
        return (lax.rem(chip + k, chips) * 2 + core, my_head)

    partner = (chip * 2 + 1 - core, my_head)

    def at_head(k):
        return (me, lax.rem(my_head + k, nh))

    def send_tile(stage, k, src, dst, device):
        copy = pltpu.make_async_remote_copy(
            src_ref=src,
            dst_ref=dst,
            send_sem=tile_send.at[stage, k],
            recv_sem=tile_recv.at[stage, k],
            device_id=device,
            device_id_type=MESH,
        )
        copy.start()
        return copy

    def send_head(stage, k, src, dst, device):
        copy = pltpu.make_async_remote_copy(
            src_ref=src,
            dst_ref=dst,
            send_sem=head_send.at[stage, k],
            recv_sem=head_recv.at[stage, k],
            device_id=device,
            device_id_type=MESH,
        )
        copy.start()
        return copy

    started = []

    def arrived(copies):
        for copy in copies:
            copy.wait_recv()
        started.extend(copies)

    barrier = pltpu.get_barrier_semaphore()
    for k in range(1, n):
        pl.semaphore_signal(barrier, inc=1, device_id=at_tile(k), device_id_type=MESH)
    for k in range(1, nh):
        pl.semaphore_signal(barrier, inc=1, device_id=at_head(k), device_id_type=MESH)

    loads = {}
    for i, (name, src, dst) in enumerate(
        (
            ("cot", cot_hbm, cot_ref),
            ("tokens", tokens_hbm, tokens_ref),
            ("gain", gain_hbm, gain_ref),
            ("qkv", qkv_hbm, qkv_ref),
            ("kpool", kpool_hbm, kpool_ref),
            ("vpool", vpool_hbm, vpool_ref),
            ("qpool", qpool_hbm, qpool_ref),
            ("skip", skip_hbm, skip_ref),
            ("proj", proj_hbm, proj_ref),
        )
    ):
        loads[name] = pltpu.make_async_copy(src, dst, load_sem.at[i])
        loads[name].start()

    order = one_hot(token_order, TILE_H * TILE_W)
    loads["cot"].wait()
    cot_all[my_head] = cot_ref[...]
    pl.semaphore_wait(barrier, n + nh - 2)
    cot_copies = [
        send_head(0, k, cot_ref, cot_all.at[my_head], at_head(k)) for k in range(1, nh)
    ]

    loads["tokens"].wait()
    tokens = mm(order, tokens_ref[...])
    center = tokens - jnp.mean(tokens, axis=-1, keepdims=True)
    inv_std = lax.rsqrt(jnp.mean(center * center, axis=-1, keepdims=True) + EPSILON)
    unit = center * inv_std
    unit_ref[...] = unit
    inv_ref[...] = jnp.broadcast_to(inv_std, inv_ref.shape)
    loads["gain"].wait()
    gain = gain_ref[...].reshape(1, wide)
    normed = (unit * gain).astype(BF16)

    for name in ("qkv", "kpool", "vpool"):
        loads[name].wait()
    kpool = kpool_ref[...].astype(F32)
    vpool = vpool_ref[...].astype(F32)

    def pool_block(field, pool):
        total = pool[0:1] * field[0:SLAB]
        for s in range(1, 16):
            total = total + pool[s : s + 1] * field[s * SLAB : (s + 1) * SLAB]
        return total

    kv_all[0, 0:SLAB, :] = pool_block(mm(normed, qkv_ref[1], (1, 1)), kpool).astype(BF16)
    kv_all[1, 0:SLAB, :] = pool_block(mm(normed, qkv_ref[2], (1, 1)), vpool).astype(BF16)

    kv_copies = [
        send_tile(
            0,
            k,
            kv_all.at[:, 0:SLAB],
            kv_all.at[:, k * SLAB : (k + 1) * SLAB],
            at_tile(k),
        )
        for k in range(1, n)
    ]

    def cell_slabs(a, b):
        return [
            (2 * a2 + b2, (2 * a + a2) * 4 + 2 * b + b2) for a2 in range(2) for b2 in range(2)
        ]

    loads["qpool"].wait()
    qpool = qpool_ref[...].astype(F32)
    field = mm(normed, qkv_ref[0], (1, 1))
    query_parts = []
    input_parts = []
    for a in range(2):
        for b in range(2):
            total = None
            whole = None
            for w, s in cell_slabs(a, b):
                term = qpool[w : w + 1] * field[s * SLAB : (s + 1) * SLAB]
                total = term if total is None else total + term
                piece = tokens[s * SLAB : (s + 1) * SLAB]
                whole = piece if whole is None else whole + piece
            query_parts.append(total)
            input_parts.append(whole)
    queries_wide = jnp.concatenate(query_parts, axis=0).astype(BF16).astype(F32)
    pooled_input = (jnp.concatenate(input_parts, axis=0) * 0.25).astype(BF16)

    cells = one_hot(cell_order, CELLS)
    cells_back = one_hot(cell_order, CELLS, transposed=True)
    loads["skip"].wait()

    own_cot = mm(cells, cot_ref[...]).astype(BF16)
    d_pooled = mm(own_cot, skip_ref[...]).astype(BF16)
    half = CELLS // 2
    dp_send[0] = d_pooled[:half]
    dp_send[1] = d_pooled[half:]
    dp_copies = [
        send_head(
            1,
            k,
            dp_send.at[lax.rem(my_head + k, nh) * 2 // nh],
            dp_recv.at[k],
            at_head(k),
        )
        for k in range(1, nh)
    ]

    loads["proj"].wait()
    arrived(cot_copies)
    full_cot = jnp.concatenate([cot_all[h] for h in range(nh)], axis=1)
    full_cot = mm(cells, full_cot).astype(BF16)
    d_attended = mm(full_cot, proj_ref[...], (1, 1)).astype(BF16).astype(F32)

    heads = chans // HEAD_DIM
    lane = lax.broadcasted_iota(jnp.int32, (CELLS, chans), 1)
    masks = [
        jnp.logical_and(lane >= h * HEAD_DIM, lane < (h + 1) * HEAD_DIM) for h in range(heads)
    ]

    def by_head(x):
        return jnp.concatenate([jnp.where(m, x, 0.0) for m in masks], axis=0).astype(BF16)

    def from_heads(x):
        total = jnp.where(masks[0], x[:CELLS], 0.0)
        for h in range(1, heads):
            total = jnp.where(masks[h], x[h * CELLS : (h + 1) * CELLS], total)
        return total

    q_rows = by_head(queries_wide)
    g_rows = by_head(d_attended)

    arrived(kv_copies)
    keys = kv_all[0]
    values = kv_all[1]
    scale = HEAD_DIM ** (-0.5)
    exp_scores = jnp.exp(mm(keys, q_rows, (1, 1)) * scale)
    row_total = jnp.sum(exp_scores, axis=0, keepdims=True)
    probs = (exp_scores / row_total).astype(BF16)
    dprobs = mm(values, g_rows, (1, 1))
    probs_wide = probs.astype(F32)
    row_delta = jnp.sum(probs_wide * dprobs, axis=0, keepdims=True)
    d_scores = (scale * probs_wide * (dprobs - row_delta)).astype(BF16)
    key_grad = mm(d_scores, q_rows)
    value_grad = mm(probs, g_rows)
    kvg_send[0] = key_grad.astype(BF16)
    kvg_send[1] = value_grad.astype(BF16)
    kvg_copies = [
        send_tile(
            1,
            k,
            kvg_send.at[:, k * SLAB : (k + 1) * SLAB],
            kvg_recv.at[:, k * SLAB : (k + 1) * SLAB],
            at_tile(n - k),
        )
        for k in range(1, n)
    ]

    attended = (from_heads(mm(probs, values, (0, 0))) + queries_wide).astype(BF16)
    head_part = mm(mm(cells_back, attended).astype(BF16), proj_ref[...])
    for h in range(nh):
        hp_send[h] = head_part[:, h * chans : (h + 1) * chans].astype(BF16)
    hp_copies = [
        send_head(2, k, hp_send.at[lax.rem(my_head + k, nh)], hp_recv.at[k], at_head(k))
        for k in range(1, nh)
    ]

    query_grad = from_heads(mm(d_scores, keys, (0, 0))) + d_attended
    spread = []
    for s in range(16):
        a, b = s // 4, s % 4
        cell = (a // 2) * 2 + b // 2
        w = (a % 2) * 2 + b % 2
        spread.append(qpool[w : w + 1] * query_grad[cell * SLAB : (cell + 1) * SLAB])
    d_projected = jnp.concatenate(spread, axis=0).astype(BF16)
    ga_send[0:chans, :] = mm(d_projected, normed, (0, 0)).astype(BF16)
    proj_part = mm(attended, full_cot, (0, 0)).astype(BF16)
    halves = proj_part.shape[1] // wide
    for i in range(halves):
        ga_send[(i + 1) * chans : (i + 2) * chans, :] = proj_part[:, i * wide : (i + 1) * wide]
    filled = (halves + 1) * chans
    if ga_send.shape[0] > filled:
        ga_send[filled:, :] = jnp.zeros((ga_send.shape[0] - filled, wide), BF16)
    half_a, half_b = chips * share_a, chips * share_b
    ga_pairs = [
        send_tile(2, 1, ga_send.at[rows((1 - core) * half_a, half_a)], ga_pair, partner)
    ]
    d_normed = mm(d_projected, qkv_ref[0])

    def fold(stage, pairs, sent, pair, part, received, share):
        arrived(pairs)
        size = chips * share
        total = sent[rows(core * size, size), :].astype(F32) + pair[...].astype(F32)
        part[...] = total.astype(BF16)
        return [
            send_tile(
                stage,
                k,
                part.at[rows(lax.rem(chip + k, chips) * share, share)],
                received.at[k],
                at_chip(k),
            )
            for k in range(1, chips)
        ]

    def place(k, share):
        from_chip = lax.rem(chip + chips - k, chips)
        return rows((core * chips + from_chip) * share, share)

    def reduce_and_share(stage, copies, part, received, out, share):
        arrived(copies)
        total = part[rows(chip * share, share), :].astype(F32)
        for k in range(1, chips):
            total = total + received[k].astype(F32)
        mine = place(0, share)
        out[mine, :] = total.astype(BF16)
        shares = [
            send_tile(stage, k, out.at[mine], out.at[mine], at_chip(k))
            for k in range(1, chips)
        ]
        relays = [send_tile(stage + 1, 0, out.at[mine], out.at[mine], partner)]
        return shares, relays

    def relay(stage, shares, relays, out, share):
        for k in range(1, chips):
            arrived(shares[k - 1 : k])
            there = place(k, share)
            relays.append(send_tile(stage, k, out.at[there], out.at[there], partner))

    ga_copies = fold(3, ga_pairs, ga_send, ga_pair, ga_part, ga_recv, share_a)

    arrived(kvg_copies)
    d_fields = []
    for j, pool, own in ((0, kpool, key_grad), (1, vpool, value_grad)):
        total = own[0:SLAB]
        for k in range(1, n):
            total = total + kvg_recv[j, k * SLAB : (k + 1) * SLAB, :].astype(F32)
        d_projected = jnp.concatenate([pool[s : s + 1] * total for s in range(16)], axis=0)
        d_fields.append(d_projected.astype(BF16))
        d_normed = d_normed + mm(d_fields[j], qkv_ref[j + 1])
    dn_send[...] = d_normed.astype(BF16)
    piece = share_h // 2
    dn_copies = [
        [
            send_head(
                3 + half,
                k,
                dn_send.at[rows(lax.rem(my_head + k, nh) * share_h + half * piece, piece)],
                dn_recv.at[k, half * piece : (half + 1) * piece],
                at_head(k),
            )
            for k in range(1, nh)
        ]
        for half in range(2)
    ]
    for j in range(2):
        gb_send[j * chans : (j + 1) * chans, :] = mm(d_fields[j], normed, (0, 0)).astype(BF16)
    filled = 2 * chans
    if gb_send.shape[0] > filled:
        gb_send[filled:, :] = jnp.zeros((gb_send.shape[0] - filled, wide), BF16)
    gb_pairs = [
        send_tile(6, 1, gb_send.at[rows((1 - core) * half_b, half_b)], gb_pair, partner)
    ]

    pooled_input = mm(cells_back, pooled_input).astype(BF16)
    skipped = mm(pooled_input, skip_ref[...], (1, 1))
    arrived(dp_copies)
    d_pooled = dp_send[my_head * 2 // nh].astype(F32)
    for k in range(1, nh):
        d_pooled = d_pooled + dp_recv[k].astype(F32)
    d_pooled = d_pooled * 0.25

    gb_copies = fold(7, gb_pairs, gb_send, gb_pair, gb_part, gb_recv, share_b)
    ga_shares, ga_relays = reduce_and_share(4, ga_copies, ga_part, ga_recv, ga_out, share_a)

    arrived(hp_copies)
    summed = hp_send[my_head].astype(F32)
    for k in range(1, nh):
        summed = summed + hp_recv[k].astype(F32)
    block_out_ref[...] = (summed + skipped).astype(BF16)

    def share_input(half):
        arrived(dn_copies[half])
        mine = rows(my_head * share_h + half * piece, piece)
        d_normed = dn_send[mine, :].astype(F32)
        for k in range(1, nh):
            d_normed = d_normed + dn_recv[k, half * piece : (half + 1) * piece, :].astype(F32)
        scaled = d_normed * gain
        own_unit = unit_ref[mine, :]
        back = inv_ref[mine, :][:, 0:1] * (
            scaled
            - jnp.mean(scaled, axis=-1, keepdims=True)
            - own_unit * jnp.mean(scaled * own_unit, axis=-1, keepdims=True)
        )
        cell = d_pooled[half * SLAB : (half + 1) * SLAB]
        ig_all[mine, :] = (back + jnp.concatenate([cell, cell], axis=0)).astype(BF16)
        return [
            send_head(5 + half, k, ig_all.at[mine], ig_all.at[mine], at_head(k))
            for k in range(1, nh)
        ]

    ig_copies = share_input(0)
    gb_shares, gb_relays = reduce_and_share(8, gb_copies, gb_part, gb_recv, gb_out, share_b)
    ig_copies += share_input(1)
    relay(5, ga_shares, ga_relays, ga_out, share_a)
    relay(9, gb_shares, gb_relays, gb_out, share_b)
    arrived(ig_copies)
    arrived(ga_relays)
    arrived(gb_relays)
    for copy in started:
        copy.wait_send()


def finish(
    block_ref, ig_ref, ga_ref, gb_ref, block_hbm, ig_hbm, qkv_hbm, proj_hbm, ig, qkv, proj, sems
):
    chans, wide = qkv.shape[1:]
    copies = []

    def put(src, dst):
        copy = pltpu.make_async_copy(src, dst, sems.at[len(copies)])
        copy.start()
        copies.append(copy)

    back = one_hot(token_order, TILE_H * TILE_W, transposed=True)
    ig[...] = mm(back, ig_ref[...]).astype(BF16)
    put(ig, ig_hbm)
    put(block_ref, block_hbm)
    for i in range(proj.shape[1] // wide):
        proj[:, i * wide : (i + 1) * wide] = ga_ref[
            (i + 1) * chans : (i + 2) * chans, :
        ].astype(F32)
    put(proj, proj_hbm)
    for j, part in enumerate(
        (ga_ref[0:chans, :], gb_ref[0:chans, :], gb_ref[chans : 2 * chans, :])
    ):
        qkv[j] = part.astype(F32)
        put(qkv.at[j], qkv_hbm.at[j])
    for copy in copies:
        copy.wait()


def share_of(total, n):
    return -(-total // (n * 16)) * 16


def local(n, nh, *operands):
    tokens, ln_gain, qkv, qpool, kpool, vpool, proj, skip, cot = operands
    count, wide = tokens.shape
    chans = qkv.shape[1]
    full = proj.shape[1]
    share_a = share_of(chans * (1 + full // wide), n)
    share_b = share_of(chans * 2, n)
    share_h = count // nh
    vmem = pl.BlockSpec(memory_space=pltpu.VMEM)
    hbm = pl.BlockSpec(memory_space=pltpu.HBM)
    outs = pl.pallas_call(
        functools.partial(kernel, n, nh, share_a, share_b),
        out_shape=(
            jax.ShapeDtypeStruct(cot.shape, BF16),
            jax.ShapeDtypeStruct(tokens.shape, BF16),
            jax.ShapeDtypeStruct((n * share_a, wide), BF16),
            jax.ShapeDtypeStruct((n * share_b, wide), BF16),
        ),
        in_specs=[hbm] * 9,
        out_specs=(vmem,) * 4,
        scratch_shapes=[pltpu.VMEM(x.shape, x.dtype) for x in operands]
        + [
            pltpu.VMEM((nh,) + cot.shape, BF16),
            pltpu.VMEM((2, n * SLAB, chans), BF16),
            pltpu.VMEM((2, n * SLAB, chans), BF16),
            pltpu.VMEM((2, n * SLAB, chans), BF16),
            pltpu.VMEM((2, CELLS // 2, wide), BF16),
            pltpu.VMEM((nh, CELLS // 2, wide), BF16),
            pltpu.VMEM((nh,) + cot.shape, BF16),
            pltpu.VMEM((nh,) + cot.shape, BF16),
            pltpu.VMEM((n * share_a, wide), BF16),
            pltpu.VMEM((n // 2 * share_a, wide), BF16),
            pltpu.VMEM((n // 2 * share_a, wide), BF16),
            pltpu.VMEM((n // 2, share_a, wide), BF16),
            pltpu.VMEM((n * share_b, wide), BF16),
            pltpu.VMEM((n // 2 * share_b, wide), BF16),
            pltpu.VMEM((n // 2 * share_b, wide), BF16),
            pltpu.VMEM((n // 2, share_b, wide), BF16),
            pltpu.VMEM((count, wide), BF16),
            pltpu.VMEM((nh, share_h, wide), BF16),
            pltpu.VMEM((count, wide), F32),
            pltpu.VMEM((count, 128), F32),
            pltpu.SemaphoreType.DMA((9,)),
            pltpu.SemaphoreType.DMA((10, n)),
            pltpu.SemaphoreType.DMA((10, n)),
            pltpu.SemaphoreType.DMA((7, nh)),
            pltpu.SemaphoreType.DMA((7, nh)),
        ],
        compiler_params=pltpu.CompilerParams(
            collective_id=0, has_side_effects=True, vmem_limit_bytes=40 * 1024 * 1024
        ),
    )(*[pltpu.with_memory_space_constraint(x, pltpu.HBM) for x in operands])
    return pl.pallas_call(
        finish,
        out_shape=(
            jax.ShapeDtypeStruct(cot.shape, BF16),
            jax.ShapeDtypeStruct(tokens.shape, BF16),
            jax.ShapeDtypeStruct(qkv.shape, F32),
            jax.ShapeDtypeStruct(proj.shape, F32),
        ),
        in_specs=[vmem] * 4,
        out_specs=(hbm,) * 4,
        scratch_shapes=[
            pltpu.VMEM(tokens.shape, BF16),
            pltpu.VMEM(qkv.shape, F32),
            pltpu.VMEM(proj.shape, F32),
            pltpu.SemaphoreType.DMA((6,)),
        ],
        compiler_params=pltpu.CompilerParams(vmem_limit_bytes=16 * 1024 * 1024),
    )(*outs)


def solution(mesh):
    placed = (
        P("tile", None),
        P(),
        P(None, "head", None),
        P(None, "head"),
        P(None, "head"),
        P(None, "head"),
        P("head", None),
        P("head", None),
        P("tile", "head"),
    )
    return jax.shard_map(
        functools.partial(local, mesh.shape["tile"], mesh.shape["head"]),
        mesh=mesh,
        in_specs=placed,
        out_specs=(P("tile", "head"), P("tile", None), P(None, "head", None), P("head", None)),
        check_vma=False,
    )
```
